32 devices in a mesh: ens: 2 (over y), gx: 8 (over z, x), gy: 2 (over core).
Axes of the slice: x: 2, y: 2, z: 4, core: 2. Of those that a mesh axis runs over, the one named last changes fastest.
Arguments:
- right_side: float32 [4, 32, 128, 128], P('ens', 'gx', 'gy'), parts along dimension 0, may hold values from -300 to 300
- cell_diag: float32 [4, 32, 128, 128], P('ens', 'gx', 'gy'), parts along dimension 0, may hold values from 11 to 15
- cell_cross: float32 [4, 32, 128, 128], P('ens', 'gx', 'gy'), parts along dimension 0, may hold values from -1 to 1
- upper_diag: float32 [6, 2, 32, 128, 128], P('ens', None, 'gx', 'gy'), parts along dimension 0, may hold values from 0.2 to 1.2
- upper_cross: float32 [6, 2, 32, 128, 128], P('ens', None, 'gx', 'gy'), parts along dimension 0, may hold values from -0.3 to 0.3
- lower_diag: float32 [6, 2, 32, 128, 128], P('ens', None, 'gx', 'gy'), parts along dimension 0, may hold values from 0.2 to 1.2
- lower_cross: float32 [6, 2, 32, 128, 128], P('ens', None, 'gx', 'gy'), parts along dimension 0, may hold values from -0.3 to 0.3
- spai_diag: float32 [4, 32, 128, 128], P('ens', 'gx', 'gy'), parts along dimension 0, may hold values from 0.06 to 0.1
- spai_cross: float32 [4, 32, 128, 128], P('ens', 'gx', 'gy'), parts along dimension 0, may hold values from -0.03 to 0.03
- perf_cell: int32 [16, 2, 256], P(('ens', 'gx'), 'gy'), parts along dimension 0, may hold values from 0 to 32767, as said below
- perf_owner: int32 [16, 2, 256], P(('ens', 'gx'), 'gy'), parts along dimension 0, may hold values from 0 to 7, as said below
- perf_well: int32 [16, 2, 256], P(('ens', 'gx'), 'gy'), parts along dimension 0, may hold values from 0 to 31
- perf_index: float32 [16, 2, 256], P(('ens', 'gx'), 'gy'), parts along dimension 0, may hold values from 0.5 to 5
- well_storage: float32 [16, 2, 32], P(('ens', 'gx'), 'gy'), parts along dimension 0, may hold values from 2 to 20
Outputs:
- adjoint: float32 [4, 32, 128, 128], P('ens', 'gx', 'gy'), parts along dimension 0
- residual: float32 [4, 32, 128, 128], P('ens', 'gx', 'gy'), parts along dimension 0
The draws below stay inside these ranges and needn't reach their ends.
There are 2 independent parts, one for each index of `ens`. The reference program is written for one: setup_inputs(seed, part) draws one part's arguments, and reference() takes and returns one part's arrays. A program takes and returns all parts, laid end to end along the dimension named above; each array names one. Nothing has to cross between parts.
Inputs may be any that keep to these rules, and one draw needn't show every extreme that they name: `perf_owner`: every perforation's owner lies within two tiles of the perforation's own gx index. Each tile names its own index exactly 128 times and any other owner at most 128 times. `perf_cell`: the perforations of one well lie in one layer and one row of the second dimension, along the first dimension.
All inputs are finite; a program needn't handle non-finite values.
Results may differ from the reference program's by a relative error of at most 0.00024.
Values sent between devices are 32-bit elements; how exact they have to be, the bound alone decides.
A program may use at most 128 MiB of HBM per device.

```python
import math
import jax
import jax.numpy as jnp
from jax import lax

CX = 4
CY = 64
NZ = 128
ITERS = 2
WELL_DEV = 32
PERF = 256
SLOT = 128
NX = 32
NY = 128
WELLS = 512
N_GX = 8
N_GY = 2


def draw_right_side(key, part):
    key = jax.random.fold_in(key, 11)
    key_noise, key_scale = jax.random.split(key)
    noise = jnp.clip(jax.random.normal(key_noise, (2, NX, NY, NZ), jnp.float32), -6.0, 6.0)
    ramp = (1.0 + 2.0 * jnp.arange(NX, dtype=jnp.float32) / max(NX - 1, 1)).reshape(1, NX, 1, 1)
    column = jnp.exp(jax.random.uniform(key_scale, (1, NX, NY, 1), jnp.float32) * math.log(10.0))
    field = noise * column * ramp
    return field.astype(jnp.float32)


def perforation_layout(key):
    tiles_x = NX // CX
    tiles_y = NY // CY
    key_owner, key_well, key_row, key_layer, key_along = jax.random.split(key, 5)
    steps_away = jnp.repeat(jnp.array([-2, -1, 1, 2], jnp.int32), SLOT)
    flat_tiles = jnp.arange(tiles_x * tiles_y, dtype=jnp.int32)

    def one_tile(tile):
        tile_key = jax.random.fold_in(key_owner, tile)
        index = tile // tiles_y
        key_pick, key_order = jax.random.split(tile_key)
        picked = steps_away[jax.random.permutation(key_pick, 4 * SLOT)]
        target = index + picked
        outside = ((target < 0) | (target >= tiles_x)).astype(jnp.int32)
        order = jnp.argsort(outside, stable=True)
        chosen = target[order][:PERF - SLOT]
        owners = jnp.concatenate([jnp.full((SLOT,), 1, jnp.int32) * index, chosen.astype(jnp.int32)])
        return owners[jax.random.permutation(key_order, PERF)]
    owners = jax.vmap(one_tile)(flat_tiles).reshape(tiles_x, tiles_y, PERF).astype(jnp.int32)
    wells = jax.random.randint(key_well, (tiles_x, tiles_y, PERF), 0, WELL_DEV).astype(jnp.int32)
    row_table = jax.random.randint(key_row, (tiles_x, tiles_y, WELL_DEV), 0, CY).astype(jnp.int32)
    layer_table = jax.random.randint(key_layer, (tiles_x, tiles_y, WELL_DEV), 0, NZ).astype(jnp.int32)
    row_of = jnp.arange(tiles_y, dtype=jnp.int32)[None, :, None]
    rows = row_table[owners, row_of, wells]
    layers = layer_table[owners, row_of, wells]
    along = jax.random.randint(key_along, (tiles_x, tiles_y, PERF), 0, CX).astype(jnp.int32)
    cells = (along * CY + rows) * NZ + layers
    return (owners, wells, cells.astype(jnp.int32))


def draw_perf_cell(key, part):
    return perforation_layout(key)[2]


def draw_perf_owner(key, part):
    return perforation_layout(key)[0]


def draw_perf_well(key, part):
    return perforation_layout(key)[1]


def levels(own_key, extent, cuts, smallest, high):
    factor_of, own = 1.0, jax.random.fold_in(own_key, 6)
    for position, blocks in cuts:
        steps = jnp.exp(jax.random.uniform(jax.random.fold_in(own, position), (blocks,), jnp.float32, smallest / len(cuts), high / len(cuts)))
        factor_of = factor_of * jnp.repeat(steps, extent[position] // blocks).reshape([-1 if axis == position else 1 for axis in range(len(extent))])
    return factor_of


def setup_inputs(seed: int = 0, part: int = 0) -> dict:
    keys = jax.random.split(jax.random.key(seed), 15)
    part_splits = jax.random.split(jax.random.fold_in(keys[14], part), 15)
    right_side = draw_right_side(jax.random.fold_in(jax.random.fold_in(keys[14], part), 71), part)
    cell_diag = jnp.clip(11.0 + 4.0 * jax.random.uniform(part_splits[1], (2, NX, NY, NZ), jnp.float32) ** levels(part_splits[1], (2, NX, NY, NZ), ((1, 8), (2, 2)), -0.2, 0.2), 11.0, 15.0)
    cell_cross = jnp.clip(jax.random.uniform(part_splits[2], (2, NX, NY, NZ), jnp.float32, -1.0, 1.0) * levels(part_splits[2], (2, NX, NY, NZ), ((1, 8), (2, 2)), -0.4, 0.0), -1.0, 1.0)
    upper_diag = jnp.clip(0.2 + 1 * jax.random.uniform(part_splits[3], (3, 2, NX, NY, NZ), jnp.float32) ** levels(part_splits[3], (3, 2, NX, NY, NZ), ((2, 8), (3, 2)), -0.2, 0.2), 0.2, 1.2)
    upper_cross = jnp.clip(jax.random.uniform(part_splits[4], (3, 2, NX, NY, NZ), jnp.float32, -0.3, 0.3) * levels(part_splits[4], (3, 2, NX, NY, NZ), ((2, 8), (3, 2)), -0.4, 0.0), -0.3, 0.3)
    lower_diag = jnp.clip(0.2 + 1 * jax.random.uniform(part_splits[5], (3, 2, NX, NY, NZ), jnp.float32) ** levels(part_splits[5], (3, 2, NX, NY, NZ), ((2, 8), (3, 2)), -0.2, 0.2), 0.2, 1.2)
    lower_cross = jnp.clip(jax.random.uniform(part_splits[6], (3, 2, NX, NY, NZ), jnp.float32, -0.3, 0.3) * levels(part_splits[6], (3, 2, NX, NY, NZ), ((2, 8), (3, 2)), -0.4, 0.0), -0.3, 0.3)
    spai_diag = jnp.clip(0.06 + 0.040000003 * jax.random.uniform(part_splits[7], (2, NX, NY, NZ), jnp.float32) ** levels(part_splits[7], (2, NX, NY, NZ), ((1, 8), (2, 2)), -0.2, 0.2), 0.06, 0.1)
    spai_cross = jnp.clip(jax.random.uniform(part_splits[8], (2, NX, NY, NZ), jnp.float32, -0.03, 0.03) * levels(part_splits[8], (2, NX, NY, NZ), ((1, 8), (2, 2)), -0.4, 0.0), -0.03, 0.03)
    perf_cell = draw_perf_cell(jax.random.fold_in(jax.random.fold_in(keys[14], part), 71), part)
    perf_owner = draw_perf_owner(jax.random.fold_in(jax.random.fold_in(keys[14], part), 71), part)
    perf_well = draw_perf_well(jax.random.fold_in(jax.random.fold_in(keys[14], part), 71), part)
    perf_index = jnp.clip(jnp.exp(math.log(5.0) - 2.3025851 * jax.random.uniform(part_splits[12], (N_GX, N_GY, PERF), jnp.float32) ** levels(part_splits[12], (N_GX, N_GY, PERF), ((0, 8), (1, 2)), -0.2, 0.2)), 0.5, 5.0)
    well_storage = jnp.clip(jnp.exp(math.log(20.0) - 2.3025851 * jax.random.uniform(part_splits[13], (N_GX, N_GY, WELL_DEV), jnp.float32) ** levels(part_splits[13], (N_GX, N_GY, WELL_DEV), ((0, 8), (1, 2)), -0.2, 0.2)), 2.0, 20.0)
    return dict(right_side=right_side, cell_diag=cell_diag, cell_cross=cell_cross, upper_diag=upper_diag, upper_cross=upper_cross, lower_diag=lower_diag, lower_cross=lower_cross, spai_diag=spai_diag, spai_cross=spai_cross, perf_cell=perf_cell, perf_owner=perf_owner, perf_well=perf_well, perf_index=perf_index, well_storage=well_storage)


def transposed(diag, cross, field):
    return jnp.stack([diag[0] * field[0] + cross[1] * field[1], cross[0] * field[0] + diag[1] * field[1]])


def below(field, axis):
    count = field.shape[axis]
    plane = jnp.zeros_like(lax.slice_in_dim(field, 0, 1, axis=axis))
    return jnp.concatenate([plane, lax.slice_in_dim(field, 0, count - 1, axis=axis)], axis=axis)


def above(field, axis):
    count = field.shape[axis]
    plane = jnp.zeros_like(lax.slice_in_dim(field, 0, 1, axis=axis))
    return jnp.concatenate([lax.slice_in_dim(field, 1, count, axis=axis), plane], axis=axis)


def reference(right_side, cell_diag, cell_cross, upper_diag, upper_cross, lower_diag, lower_cross, spai_diag, spai_cross, perf_cell, perf_owner, perf_well, perf_index, well_storage):
    tile_x = jnp.arange(N_GX, dtype=jnp.int32)[:, None, None]
    tile_y = jnp.arange(N_GY, dtype=jnp.int32)[None, :, None]
    cell_x = tile_x * CX + perf_cell // (CY * NZ)
    cell_y = tile_y * CY + (perf_cell // NZ) % CY
    cell_z = perf_cell % NZ
    flat_cell = ((cell_x * NY + cell_y) * NZ + cell_z).reshape(-1).astype(jnp.int32)
    well_id = ((perf_owner * N_GY + tile_y) * WELL_DEV + perf_well).reshape(-1).astype(jnp.int32)
    weights = perf_index.reshape(-1)
    totals = jax.ops.segment_sum(weights, well_id, num_segments=WELLS)
    denom = totals + well_storage.reshape(-1)

    def well_term(field):
        flat = field.reshape(2, -1)
        values = flat[:, flat_cell]
        sums = jax.ops.segment_sum((weights * values).T, well_id, num_segments=WELLS)
        means = sums / denom[:, None]
        term = weights * (values - means[well_id].T)
        return jnp.zeros_like(flat).at[:, flat_cell].add(term).reshape(field.shape)

    def apply(field):
        total = transposed(cell_diag, cell_cross, field)
        for dim in range(3):
            axis = dim + 1
            total = total - below(transposed(upper_diag[dim], upper_cross[dim], field), axis)
            total = total - transposed(lower_diag[dim], lower_cross[dim], above(field, axis))
        return total + well_term(field)

    def precondition(field):
        return transposed(spai_diag, spai_cross, field)

    adjoint = jnp.zeros_like(right_side)
    residual = right_side
    shadow = right_side
    direction = jnp.zeros_like(right_side)
    image = jnp.zeros_like(right_side)
    rho, alpha, omega = 1.0, 1.0, 1.0
    for step in range(ITERS):
        rho_new = jnp.sum(shadow * residual)
        beta = (rho_new / rho) * (alpha / omega)
        direction = residual + beta * (direction - omega * image)
        lifted = precondition(direction)
        image = apply(lifted)
        alpha = rho_new / jnp.sum(shadow * image)
        half = residual - alpha * image
        half_lifted = precondition(half)
        turned = apply(half_lifted)
        omega = jnp.sum(turned * half) / jnp.sum(turned * turned)
        adjoint = adjoint + alpha * lifted + omega * half_lifted
        residual = half - omega * turned
        rho = rho_new
    return adjoint, residual
```

```python
import functools

import jax
import jax.numpy as jnp
from jax import lax
from jax.experimental import pallas as pl
from jax.experimental.pallas import tpu as pltpu
from jax.sharding import PartitionSpec as P

MESH = pl.DeviceIdType.MESH
ITERS = 2
POWERS = 2 * ITERS
SHIFT = 1.0
RING = 8
REACH = 4
F32 = jnp.float32
BF16 = jnp.bfloat16


def parts(value, count):
    pieces = []
    for _ in range(count):
        piece = value.astype(BF16)
        pieces.append(piece)
        value = value - piece.astype(F32)
    return pieces


def rows_dot(first, second):
    return lax.dot_general(first, second, (((1,), (1,)), ((), ())), preferred_element_type=F32)


def combine(terms, vectors):
    total = None
    for term, vector in zip(terms, vectors):
        if term is None:
            continue
        piece = term * vector
        total = piece if total is None else total + piece
    return total


def add(first, second):
    if first is None:
        return second
    if second is None:
        return first
    return first + second


def scale(factor, terms):
    return [None if t is None else factor * t for t in terms]


def plus(first, second):
    return [add(a, b) for a, b in zip(first, second)]


def advance(terms):
    moved = [None] + list(terms[:-1])
    return plus(moved, scale(SHIFT, terms))


def bicgstab_terms(gram):
    def product(first, second):
        total = None
        for i, a in enumerate(first):
            for j, b in enumerate(second):
                if a is not None and b is not None:
                    total = add(total, a * b * gram[(min(i, j), max(i, j))])
        return total

    count = POWERS + 1
    one = jnp.ones_like(gram[(0, 0)])
    shadow = [one] + [None] * (count - 1)
    residual = list(shadow)
    adjoint = [None] * count
    direction = image = None
    rho = alpha = omega = one
    for step in range(ITERS):
        rho_new = product(shadow, residual)
        if step == 0:
            direction = residual
        else:
            beta = rho_new / rho * (alpha / omega)
            direction = plus(residual, scale(beta, plus(direction, scale(-omega, image))))
        image = advance(direction)
        alpha = rho_new / product(shadow, image)
        half = plus(residual, scale(-alpha, image))
        turned = advance(half)
        omega = product(turned, half) / product(turned, turned)
        adjoint = plus(adjoint, plus(scale(alpha, direction), scale(omega, half)))
        residual = plus(half, scale(-omega, turned))
        rho = rho_new
    return adjoint, residual


def kernel(
    peers,
    rhs,
    cell_diag,
    cell_cross,
    up_diag,
    up_cross,
    low_diag,
    low_cross,
    spai_diag,
    spai_cross,
    perf_cell,
    perf_owner,
    perf_well,
    perf_index,
    storage,
    adjoint_out,
    residual_out,
    basis,
    lifted,
    diag,
    spread,
    mask,
    denom,
    totals,
    up_send,
    up_recv,
    down_recv,
    y_send,
    y_recv,
    well_send,
    well_recv,
    dots,
    dots_all,
    halo_send_sem,
    halo_recv_sem,
    well_send_sem,
    well_recv_sem,
    dots_send_sem,
    dots_recv_sem,
):
    gx, gy = lax.axis_index("gx"), lax.axis_index("gy")
    everyone = peers * 2
    me = gx * 2 + gy
    _, width, height, depth = rhs.shape
    rows = width * height
    lanes = perf_cell.shape[-1]
    owned = storage.shape[-1]
    buckets = RING * owned

    well_recv[...] = jnp.zeros_like(well_recv)
    barrier = pltpu.get_barrier_semaphore()
    for step in range(1, everyone):
        other = lax.rem(me + step, everyone)
        pl.semaphore_signal(
            barrier, 1, device_id={"gx": other // 2, "gy": other % 2}, device_id_type=MESH
        )

    cells = perf_cell[0]
    bucket_of = (perf_owner[0] & (RING - 1)) * owned + perf_well[0]
    row_of, layer_of = (cells // depth, cells % depth)
    weights = perf_index[0]
    in_row = lax.broadcasted_iota(jnp.int32, (rows, lanes), 0) == row_of
    in_bucket = lax.broadcasted_iota(jnp.int32, (buckets, lanes), 0) == bucket_of
    in_layer = lax.broadcasted_iota(jnp.int32, (depth, lanes), 0) == layer_of
    hot_row = in_row.astype(F32).astype(BF16)
    hot_bucket = in_bucket.astype(F32).astype(BF16)
    hot_layer = in_layer.astype(F32).astype(BF16)
    spread_now = jnp.zeros((rows, buckets), F32)
    extra = jnp.zeros((rows, depth), F32)
    for piece in parts(weights, 3):
        piece = piece.astype(F32)
        spread_now += rows_dot(hot_row, jnp.where(in_bucket, piece, 0.0).astype(BF16))
        extra += rows_dot(hot_row, jnp.where(in_layer, piece, 0.0).astype(BF16))
    spread[...] = spread_now
    layer_of_bucket = jnp.minimum(rows_dot(hot_bucket, hot_layer), 1.0).astype(BF16)
    bucket_of_layer = jnp.minimum(rows_dot(hot_layer, hot_bucket), 1.0).astype(BF16)
    layer_twice = jnp.concatenate([layer_of_bucket, layer_of_bucket], axis=0)
    bucket_twice = jnp.concatenate([bucket_of_layer, bucket_of_layer], axis=0)
    for c in range(2):
        for x in range(width):
            diag[c, x] = cell_diag[c, x] + extra[x * height : (x + 1) * height]

    place = lax.broadcasted_iota(jnp.int32, (owned, buckets), 1)
    slot = lax.broadcasted_iota(jnp.int32, (owned, buckets), 0)
    mine = (place // owned == (gx & (RING - 1))) & (place % owned == slot)
    stored = jnp.zeros((8, buckets), F32)
    for piece in parts(jnp.broadcast_to(storage[0], (8, owned)), 3):
        stored += jnp.dot(piece, mine.astype(F32).astype(BF16), preferred_element_type=F32)
    weight_sums = jnp.sum(spread_now, axis=0, keepdims=True) + stored[:1]

    tile_row = lax.broadcasted_iota(jnp.int32, (8, 128), 0)
    tile_lane = lax.broadcasted_iota(jnp.int32, (8, 128), 1)
    residue = ((tile_row % 2) * 128 + tile_lane) // owned
    here = (residue - gx + 2) & (RING - 1)
    for k in range(2 * REACH + 1):
        away = k - REACH
        there = (residue - gx - away + 2) & (RING - 1)
        same = (here < 5) & (there < 5) & (here == there + away)
        mask[k] = same.astype(F32)

    lane = lax.broadcasted_iota(jnp.int32, (height, depth), 1)
    row = lax.broadcasted_iota(jnp.int32, (height, depth), 0)
    first_lane, last_lane = (lane == 0, lane == depth - 1)
    first_row, last_row = (row == 0, row == height - 1)

    pl.semaphore_wait(barrier, everyone - 1)

    def vector(k):
        return rhs if k == 0 else basis.at[k - 1]

    def start_wells(step):
        for k in range(2 * REACH + 1):
            if k == REACH:
                continue
            away = REACH - k

            @pl.when((gx + away >= 0) & (gx + away < peers))
            def _():
                pltpu.make_async_remote_copy(
                    src_ref=well_send.at[step],
                    dst_ref=well_recv.at[step, k],
                    send_sem=well_send_sem.at[step, k],
                    recv_sem=well_recv_sem.at[step, k],
                    device_id={"gx": gx + away},
                    device_id_type=MESH,
                ).start()

    def well_copy(step, k):
        return pltpu.make_async_remote_copy(
            src_ref=well_send.at[step],
            dst_ref=well_recv.at[step, k],
            send_sem=well_send_sem.at[step, k],
            recv_sem=well_recv_sem.at[step, k],
            device_id={"gx": gx},
            device_id_type=MESH,
        )

    def halo_copy(step, kind):
        src, dst, target = [
            (up_send.at[step], up_recv.at[step], {"gx": gx + 1}),
            (lifted.at[step, :, 0], down_recv.at[step], {"gx": gx - 1}),
            (y_send.at[step], y_recv.at[step], {"gy": 1 - gy}),
        ][kind]
        return pltpu.make_async_remote_copy(
            src_ref=src,
            dst_ref=dst,
            send_sem=halo_send_sem.at[step, kind],
            recv_sem=halo_recv_sem.at[step, kind],
            device_id=target,
            device_id_type=MESH,
        )

    def block(diag_ref, cross_ref, at, f0, f1):
        d0, d1 = (diag_ref[(*at[0], 0, *at[1])], diag_ref[(*at[0], 1, *at[1])])
        c0, c1 = (cross_ref[(*at[0], 0, *at[1])], cross_ref[(*at[0], 1, *at[1])])
        return (d0 * f0 + c1 * f1, c0 * f0 + d1 * f1)

    def add_dots(k):
        sums = [jnp.zeros((8, depth), F32) for _ in range(k + 1)]
        for c in range(2):
            for x in range(width):
                last = vector(k)[c, x]
                for j in range(k + 1):
                    other = last if j == k else vector(j)[c, x]
                    sums[j] += jnp.sum((last * other).reshape(height // 8, 8, depth), axis=0)
        for j in range(k + 1):
            at = k * (k + 1) // 2 + j
            dots[at : at + 1, :] = jnp.sum(sums[j], axis=0, keepdims=True)

    for step in range(POWERS):
        source = vector(step)

        def lift(x):
            f0, f1 = block(spai_diag, spai_cross, ((), (x,)), source[0, x], source[1, x])
            lifted[step, 0, x] = f0
            lifted[step, 1, x] = f1
            return f0, f1

        lift(0)

        @pl.when(gx > 0)
        def _():
            halo_copy(step, 1).start()

        f0, f1 = lift(width - 1)
        p0, p1 = block(up_diag, up_cross, ((0,), (width - 1,)), f0, f1)
        up_send[step, 0] = p0
        up_send[step, 1] = p1

        @pl.when(gx < peers - 1)
        def _():
            halo_copy(step, 0).start()

        for x in range(1, width - 1):
            lift(x)

        @pl.when(gy == 0)
        def _():
            at = slice(height - 1, height)
            for x in range(width):
                p0, p1 = block(
                    up_diag,
                    up_cross,
                    ((1,), (x, at)),
                    lifted[step, 0, x, at],
                    lifted[step, 1, x, at],
                )
                y_send[step, x : x + 1] = p0
                y_send[step, width + x : width + x + 1] = p1

        @pl.when(gy == 1)
        def _():
            for x in range(width):
                for c in range(2):
                    y_send[step, c * width + x : c * width + x + 1] = lifted[step, c, x, 0:1]

        halo_copy(step, 2).start()

        for c in range(2):
            field = lifted[step, c].reshape(rows, depth)
            picked = jnp.dot(
                jnp.concatenate(parts(field, 2), axis=1),
                bucket_twice,
                preferred_element_type=F32,
            )
            sums = jnp.sum(picked * spread[...], axis=0, keepdims=True)
            well_send[step, 2 * c : 2 * c + 1] = sums[:, :128]
            well_send[step, 2 * c + 1 : 2 * c + 2] = sums[:, 128:]
        well_send[step, 4:5] = weight_sums[:, :128]
        well_send[step, 5:6] = weight_sums[:, 128:]
        well_send[step, 6:8] = jnp.zeros((2, 128), F32)
        start_wells(step)

        carry = None
        for x in range(width):
            f0, f1 = (lifted[step, 0, x], lifted[step, 1, x])
            here = ((), (x,))
            a0, a1 = block(diag, cell_cross, here, f0, f1)
            a0 -= SHIFT * source[0, x]
            a1 -= SHIFT * source[1, x]
            if carry is not None:
                a0 -= carry[0]
                a1 -= carry[1]
            if x < width - 1:
                carry = block(up_diag, up_cross, ((0,), (x,)), f0, f1)
                b0, b1 = block(
                    low_diag, low_cross, ((0,), (x,)), lifted[step, 0, x + 1], lifted[step, 1, x + 1]
                )
                a0 -= b0
                a1 -= b1
            y_up = block(up_diag, up_cross, ((1,), (x,)), f0, f1)
            a0 -= jnp.where(first_row, 0.0, pltpu.roll(y_up[0], 1, 0))
            a1 -= jnp.where(first_row, 0.0, pltpu.roll(y_up[1], 1, 0))
            next0 = jnp.where(last_row, 0.0, pltpu.roll(f0, height - 1, 0))
            next1 = jnp.where(last_row, 0.0, pltpu.roll(f1, height - 1, 0))
            b0, b1 = block(low_diag, low_cross, ((1,), (x,)), next0, next1)
            a0 -= b0
            a1 -= b1
            z_up = block(up_diag, up_cross, ((2,), (x,)), f0, f1)
            a0 -= jnp.where(first_lane, 0.0, pltpu.roll(z_up[0], 1, 1))
            a1 -= jnp.where(first_lane, 0.0, pltpu.roll(z_up[1], 1, 1))
            next0 = jnp.where(last_lane, 0.0, pltpu.roll(f0, depth - 1, 1))
            next1 = jnp.where(last_lane, 0.0, pltpu.roll(f1, depth - 1, 1))
            b0, b1 = block(low_diag, low_cross, ((2,), (x,)), next0, next1)
            basis[step, 0, x] = a0 - b0
            basis[step, 1, x] = a1 - b1
        add_dots(step)

        for k in range(2 * REACH + 1):
            if k == REACH:
                continue
            away = k - REACH

            @pl.when((gx + away >= 0) & (gx + away < peers))
            def _():
                well_copy(step, k).wait_recv()

        total = well_send[step]
        for k in range(2 * REACH + 1):
            if k != REACH:
                total += mask[k] * well_recv[step, k]
        if step == 0:
            totals[...] = total
            for r in range(4):
                below = totals[4 + r % 2 : 5 + r % 2]
                denom[r : r + 1] = jnp.where(below > 0.0, below, 1.0)
        means = total[:4] / denom[...]
        for c in range(2):
            mean = jnp.concatenate([means[2 * c : 2 * c + 1], means[2 * c + 1 : 2 * c + 2]], axis=1)
            taken = jnp.concatenate(parts(mean * spread[...], 2), axis=1)
            taken = jnp.dot(taken, layer_twice, preferred_element_type=F32)
            for x in range(width):
                basis[step, c, x] -= taken[x * height : (x + 1) * height]

        halo_copy(step, 2).wait_recv()

        @pl.when(gy == 0)
        def _():
            at = slice(height - 1, height)
            for x in range(width):
                f0, f1 = (y_recv[step, x : x + 1], y_recv[step, width + x : width + x + 1])
                b0, b1 = block(low_diag, low_cross, ((1,), (x, at)), f0, f1)
                basis[step, 0, x, at] -= b0
                basis[step, 1, x, at] -= b1

        @pl.when(gy == 1)
        def _():
            for x in range(width):
                for c in range(2):
                    at = c * width + x
                    basis[step, c, x, 0:1] -= y_recv[step, at : at + 1]

        @pl.when(gx > 0)
        def _():
            halo_copy(step, 0).wait_recv()
            for c in range(2):
                basis[step, c, 0] -= up_recv[step, c]

        @pl.when(gx < peers - 1)
        def _():
            halo_copy(step, 1).wait_recv()
            x = width - 1
            f0, f1 = (down_recv[step, 0], down_recv[step, 1])
            b0, b1 = block(low_diag, low_cross, ((0,), (x,)), f0, f1)
            basis[step, 0, x] -= b0
            basis[step, 1, x] -= b1

    add_dots(POWERS)
    dots[15:16, :] = jnp.zeros((1, depth), F32)

    def dots_copy(index, other):
        return pltpu.make_async_remote_copy(
            src_ref=dots,
            dst_ref=dots_all.at[index],
            send_sem=dots_send_sem.at[index],
            recv_sem=dots_recv_sem.at[index],
            device_id={"gx": other // 2, "gy": other % 2},
            device_id_type=MESH,
        )

    for step in range(1, everyone):
        other = lax.rem(me + step, everyone)
        pltpu.make_async_remote_copy(
            src_ref=dots,
            dst_ref=dots_all.at[me],
            send_sem=dots_send_sem.at[step],
            recv_sem=dots_recv_sem.at[me],
            device_id={"gx": other // 2, "gy": other % 2},
            device_id_type=MESH,
        ).start()
    dots_all[me] = dots[...]
    for step in range(1, everyone):
        other = lax.rem(me + step, everyone)
        dots_copy(other, other).wait_recv()
    gathered = jnp.sum(dots_all[...], axis=0)
    gathered = jnp.broadcast_to(jnp.sum(gathered, axis=1, keepdims=True), gathered.shape)
    gram = {}
    for k in range(POWERS + 1):
        for j in range(k + 1):
            at = k * (k + 1) // 2 + j
            gram[(j, k)] = gathered[at : at + 1, :]
    adjoint, residual = bicgstab_terms(gram)

    for x in range(width):
        fields = []
        for c in range(2):
            values = [vector(k)[c, x] for k in range(POWERS + 1)]
            residual_out[c, x] = combine(residual, values)
            fields.append(combine(adjoint, values))
        f0, f1 = block(spai_diag, spai_cross, ((), (x,)), *fields)
        adjoint_out[0, x] = f0
        adjoint_out[1, x] = f1

    for step in range(POWERS):

        @pl.when(gx < peers - 1)
        def _():
            halo_copy(step, 0).wait_send()

        @pl.when(gx > 0)
        def _():
            halo_copy(step, 1).wait_send()

        halo_copy(step, 2).wait_send()
        for k in range(2 * REACH + 1):
            if k == REACH:
                continue
            away = REACH - k

            @pl.when((gx + away >= 0) & (gx + away < peers))
            def _():
                well_copy(step, k).wait_send()

    for step in range(1, everyone):
        dots_copy(step, me).wait_send()


def shards(peers, *args):
    rhs = args[0]
    _, width, height, depth = rhs.shape
    owned = args[-1].shape[-1]
    buckets = RING * owned
    rows = width * height
    everyone = peers * 2
    plane = (POWERS, 2, height, depth)
    wells = 2 * REACH + 1
    vmem = pl.BlockSpec(memory_space=pltpu.VMEM)
    return pl.pallas_call(
        functools.partial(kernel, peers),
        out_shape=[jax.ShapeDtypeStruct(rhs.shape, F32)] * 2,
        in_specs=[vmem] * len(args),
        out_specs=[vmem] * 2,
        scratch_shapes=[
            pltpu.VMEM((POWERS, 2, width, height, depth), F32),
            pltpu.VMEM((POWERS, 2, width, height, depth), F32),
            pltpu.VMEM((2, width, height, depth), F32),
            pltpu.VMEM((rows, buckets), F32),
            pltpu.VMEM((wells, 8, 128), F32),
            pltpu.VMEM((4, 128), F32),
            pltpu.VMEM((8, 128), F32),
            pltpu.VMEM(plane, F32),
            pltpu.VMEM(plane, F32),
            pltpu.VMEM(plane, F32),
            pltpu.VMEM((POWERS, 2 * width, depth), F32),
            pltpu.VMEM((POWERS, 2 * width, depth), F32),
            pltpu.VMEM((POWERS, 8, 128), F32),
            pltpu.VMEM((POWERS, wells, 8, 128), F32),
            pltpu.VMEM((16, depth), F32),
            pltpu.VMEM((everyone, 16, depth), F32),
            pltpu.SemaphoreType.DMA((POWERS, 3)),
            pltpu.SemaphoreType.DMA((POWERS, 3)),
            pltpu.SemaphoreType.DMA((POWERS, wells)),
            pltpu.SemaphoreType.DMA((POWERS, wells)),
            pltpu.SemaphoreType.DMA((everyone,)),
            pltpu.SemaphoreType.DMA((everyone,)),
        ],
        compiler_params=pltpu.CompilerParams(
            collective_id=0, has_side_effects=True, vmem_limit_bytes=40 * 1024 * 1024
        ),
    )(*args)


def solution(mesh):
    cell = P("ens", "gx", "gy", None)
    coupling = P("ens", None, "gx", "gy", None)
    tile = P(("ens", "gx"), "gy", None)
    in_specs = (cell,) * 3 + (coupling,) * 4 + (cell,) * 2 + (tile,) * 5
    return jax.shard_map(
        functools.partial(shards, mesh.shape["gx"]),
        mesh=mesh,
        in_specs=in_specs,
        out_specs=(cell, cell),
        check_vma=False,
    )
```

```python
import functools

import jax
import jax.numpy as jnp
from jax import lax
from jax.experimental import pallas as pl
from jax.experimental.pallas import tpu as pltpu
from jax.sharding import PartitionSpec as P

MESH = pl.DeviceIdType.MESH
ITERS = 2
POWERS = 2 * ITERS
SHIFT = 1.0
RING = 8
REACH = 4
F32 = jnp.float32
BF16 = jnp.bfloat16


def parts(value, count):
    pieces = []
    for _ in range(count):
        piece = value.astype(BF16)
        pieces.append(piece)
        value = value - piece.astype(F32)
    return pieces


def rows_dot(first, second):
    return lax.dot_general(first, second, (((1,), (1,)), ((), ())), preferred_element_type=F32)


def combine(terms, vectors):
    total = None
    for term, vector in zip(terms, vectors):
        if term is None:
            continue
        piece = term * vector
        total = piece if total is None else total + piece
    return total


def add(first, second):
    if first is None:
        return second
    if second is None:
        return first
    return first + second


def scale(factor, terms):
    return [None if t is None else factor * t for t in terms]


def plus(first, second):
    return [add(a, b) for a, b in zip(first, second)]


def advance(terms):
    moved = [None] + list(terms[:-1])
    return plus(moved, scale(SHIFT, terms))


def bicgstab_terms(gram):
    def product(first, second):
        total = None
        for i, a in enumerate(first):
            for j, b in enumerate(second):
                if a is not None and b is not None:
                    total = add(total, a * b * gram[(min(i, j), max(i, j))])
        return total

    count = POWERS + 1
    one = jnp.ones_like(gram[(0, 0)])
    shadow = [one] + [None] * (count - 1)
    residual = list(shadow)
    adjoint = [None] * count
    direction = image = None
    rho = alpha = omega = one
    for step in range(ITERS):
        rho_new = product(shadow, residual)
        if step == 0:
            direction = residual
        else:
            beta = rho_new / rho * (alpha / omega)
            direction = plus(residual, scale(beta, plus(direction, scale(-omega, image))))
        image = advance(direction)
        alpha = rho_new / product(shadow, image)
        half = plus(residual, scale(-alpha, image))
        turned = advance(half)
        omega = product(turned, half) / product(turned, turned)
        adjoint = plus(adjoint, plus(scale(alpha, direction), scale(omega, half)))
        residual = plus(half, scale(-omega, turned))
        rho = rho_new
    return adjoint, residual


def kernel(
    peers,
    *refs,
):
    inputs, (adjoint_out, residual_out) = (refs[:14], refs[14:16])
    held, load_sem, refs = (refs[16:30], refs[30], refs[31:])
    run(peers, inputs, held, load_sem, adjoint_out, residual_out, *refs)


def run(
    peers,
    inputs,
    held,
    load_sem,
    adjoint_out,
    residual_out,
    basis,
    lifted,
    diag,
    spread,
    mask,
    denom,
    totals,
    up_send,
    up_recv,
    down_recv,
    y_send,
    y_recv,
    well_send,
    well_recv,
    dots,
    dots_all,
    halo_send_sem,
    halo_recv_sem,
    well_send_sem,
    well_recv_sem,
    dots_send_sem,
    dots_recv_sem,
):
    rhs, cell_diag, cell_cross, up_diag, up_cross, low_diag, low_cross = held[:7]
    spai_diag, spai_cross, perf_cell, perf_owner, perf_well, perf_index, storage = held[7:]
    loads = [pltpu.make_async_copy(inputs[k], held[k], load_sem.at[k]) for k in range(14)]
    for k in (9, 10, 11, 12, 13, 0, 7, 8, 3, 4, 1, 2, 5, 6):
        loads[k].start()

    def ready(*which):
        for k in which:
            loads[k].wait()

    gx, gy = lax.axis_index("gx"), lax.axis_index("gy")
    everyone = peers * 2
    me = gx * 2 + gy
    _, width, height, depth = rhs.shape
    rows = width * height
    lanes = perf_cell.shape[-1]
    owned = storage.shape[-1]
    buckets = RING * owned

    well_recv[...] = jnp.zeros_like(well_recv)
    barrier = pltpu.get_barrier_semaphore()
    for step in range(1, everyone):
        other = lax.rem(me + step, everyone)
        pl.semaphore_signal(
            barrier, 1, device_id={"gx": other // 2, "gy": other % 2}, device_id_type=MESH
        )

    ready(9, 10, 11, 12, 13)
    cells = perf_cell[0]
    bucket_of = (perf_owner[0] & (RING - 1)) * owned + perf_well[0]
    row_of, layer_of = (cells // depth, cells % depth)
    weights = perf_index[0]
    in_row = lax.broadcasted_iota(jnp.int32, (rows, lanes), 0) == row_of
    in_bucket = lax.broadcasted_iota(jnp.int32, (buckets, lanes), 0) == bucket_of
    in_layer = lax.broadcasted_iota(jnp.int32, (depth, lanes), 0) == layer_of
    hot_row = in_row.astype(F32).astype(BF16)
    hot_bucket = in_bucket.astype(F32).astype(BF16)
    hot_layer = in_layer.astype(F32).astype(BF16)
    spread_now = jnp.zeros((rows, buckets), F32)
    extra = jnp.zeros((rows, depth), F32)
    for piece in parts(weights, 3):
        piece = piece.astype(F32)
        spread_now += rows_dot(hot_row, jnp.where(in_bucket, piece, 0.0).astype(BF16))
        extra += rows_dot(hot_row, jnp.where(in_layer, piece, 0.0).astype(BF16))
    spread[...] = spread_now
    layer_of_bucket = jnp.minimum(rows_dot(hot_bucket, hot_layer), 1.0).astype(BF16)
    bucket_of_layer = jnp.minimum(rows_dot(hot_layer, hot_bucket), 1.0).astype(BF16)
    layer_twice = jnp.concatenate([layer_of_bucket, layer_of_bucket], axis=0)
    bucket_twice = jnp.concatenate([bucket_of_layer, bucket_of_layer], axis=0)
    ready(1)
    for c in range(2):
        for x in range(width):
            diag[c, x] = cell_diag[c, x] + extra[x * height : (x + 1) * height]

    place = lax.broadcasted_iota(jnp.int32, (owned, buckets), 1)
    slot = lax.broadcasted_iota(jnp.int32, (owned, buckets), 0)
    mine = (place // owned == (gx & (RING - 1))) & (place % owned == slot)
    stored = jnp.zeros((8, buckets), F32)
    for piece in parts(jnp.broadcast_to(storage[0], (8, owned)), 3):
        stored += jnp.dot(piece, mine.astype(F32).astype(BF16), preferred_element_type=F32)
    weight_sums = jnp.sum(spread_now, axis=0, keepdims=True) + stored[:1]

    tile_row = lax.broadcasted_iota(jnp.int32, (8, 128), 0)
    tile_lane = lax.broadcasted_iota(jnp.int32, (8, 128), 1)
    residue = ((tile_row % 2) * 128 + tile_lane) // owned
    here = (residue - gx + 2) & (RING - 1)
    for k in range(2 * REACH + 1):
        away = k - REACH
        there = (residue - gx - away + 2) & (RING - 1)
        same = (here < 5) & (there < 5) & (here == there + away)
        mask[k] = same.astype(F32)

    lane = lax.broadcasted_iota(jnp.int32, (height, depth), 1)
    row = lax.broadcasted_iota(jnp.int32, (height, depth), 0)
    first_lane, last_lane = (lane == 0, lane == depth - 1)
    first_row, last_row = (row == 0, row == height - 1)

    ready(0, 7, 8)
    pl.semaphore_wait(barrier, everyone - 1)

    def vector(k):
        return rhs if k == 0 else basis.at[k - 1]

    def start_wells(step):
        for k in range(2 * REACH + 1):
            if k == REACH:
                continue
            away = REACH - k

            @pl.when((gx + away >= 0) & (gx + away < peers))
            def _():
                pltpu.make_async_remote_copy(
                    src_ref=well_send.at[step],
                    dst_ref=well_recv.at[step, k],
                    send_sem=well_send_sem.at[step, k],
                    recv_sem=well_recv_sem.at[step, k],
                    device_id={"gx": gx + away},
                    device_id_type=MESH,
                ).start()

    def well_copy(step, k):
        return pltpu.make_async_remote_copy(
            src_ref=well_send.at[step],
            dst_ref=well_recv.at[step, k],
            send_sem=well_send_sem.at[step, k],
            recv_sem=well_recv_sem.at[step, k],
            device_id={"gx": gx},
            device_id_type=MESH,
        )

    def halo_copy(step, kind):
        src, dst, target = [
            (up_send.at[step], up_recv.at[step], {"gx": gx + 1}),
            (lifted.at[step, :, 0], down_recv.at[step], {"gx": gx - 1}),
            (y_send.at[step], y_recv.at[step], {"gy": 1 - gy}),
        ][kind]
        return pltpu.make_async_remote_copy(
            src_ref=src,
            dst_ref=dst,
            send_sem=halo_send_sem.at[step, kind],
            recv_sem=halo_recv_sem.at[step, kind],
            device_id=target,
            device_id_type=MESH,
        )

    def block(diag_ref, cross_ref, at, f0, f1):
        d0, d1 = (diag_ref[(*at[0], 0, *at[1])], diag_ref[(*at[0], 1, *at[1])])
        c0, c1 = (cross_ref[(*at[0], 0, *at[1])], cross_ref[(*at[0], 1, *at[1])])
        return (d0 * f0 + c1 * f1, c0 * f0 + d1 * f1)

    def add_dots(k):
        sums = [jnp.zeros((8, depth), F32) for _ in range(k + 1)]
        for c in range(2):
            for x in range(width):
                last = vector(k)[c, x]
                for j in range(k + 1):
                    other = last if j == k else vector(j)[c, x]
                    sums[j] += jnp.sum((last * other).reshape(height // 8, 8, depth), axis=0)
        for j in range(k + 1):
            at = k * (k + 1) // 2 + j
            dots[at : at + 1, :] = jnp.sum(sums[j], axis=0, keepdims=True)

    for step in range(POWERS):
        source = vector(step)

        def lift(x):
            f0, f1 = block(spai_diag, spai_cross, ((), (x,)), source[0, x], source[1, x])
            lifted[step, 0, x] = f0
            lifted[step, 1, x] = f1
            return f0, f1

        lift(0)

        @pl.when(gx > 0)
        def _():
            halo_copy(step, 1).start()

        f0, f1 = lift(width - 1)
        if step == 0:
            ready(3, 4)
        p0, p1 = block(up_diag, up_cross, ((0,), (width - 1,)), f0, f1)
        up_send[step, 0] = p0
        up_send[step, 1] = p1

        @pl.when(gx < peers - 1)
        def _():
            halo_copy(step, 0).start()

        for x in range(1, width - 1):
            lift(x)

        @pl.when(gy == 0)
        def _():
            at = slice(height - 1, height)
            for x in range(width):
                p0, p1 = block(
                    up_diag,
                    up_cross,
                    ((1,), (x, at)),
                    lifted[step, 0, x, at],
                    lifted[step, 1, x, at],
                )
                y_send[step, x : x + 1] = p0
                y_send[step, width + x : width + x + 1] = p1

        @pl.when(gy == 1)
        def _():
            for x in range(width):
                for c in range(2):
                    y_send[step, c * width + x : c * width + x + 1] = lifted[step, c, x, 0:1]

        halo_copy(step, 2).start()

        for c in range(2):
            field = lifted[step, c].reshape(rows, depth)
            picked = jnp.dot(
                jnp.concatenate(parts(field, 2), axis=1),
                bucket_twice,
                preferred_element_type=F32,
            )
            sums = jnp.sum(picked * spread[...], axis=0, keepdims=True)
            well_send[step, 2 * c : 2 * c + 1] = sums[:, :128]
            well_send[step, 2 * c + 1 : 2 * c + 2] = sums[:, 128:]
        well_send[step, 4:5] = weight_sums[:, :128]
        well_send[step, 5:6] = weight_sums[:, 128:]
        well_send[step, 6:8] = jnp.zeros((2, 128), F32)
        start_wells(step)

        if step == 0:
            ready(2, 5, 6)
        carry = None
        for x in range(width):
            f0, f1 = (lifted[step, 0, x], lifted[step, 1, x])
            here = ((), (x,))
            a0, a1 = block(diag, cell_cross, here, f0, f1)
            a0 -= SHIFT * source[0, x]
            a1 -= SHIFT * source[1, x]
            if carry is not None:
                a0 -= carry[0]
                a1 -= carry[1]
            if x < width - 1:
                carry = block(up_diag, up_cross, ((0,), (x,)), f0, f1)
                b0, b1 = block(
                    low_diag, low_cross, ((0,), (x,)), lifted[step, 0, x + 1], lifted[step, 1, x + 1]
                )
                a0 -= b0
                a1 -= b1
            y_up = block(up_diag, up_cross, ((1,), (x,)), f0, f1)
            a0 -= jnp.where(first_row, 0.0, pltpu.roll(y_up[0], 1, 0))
            a1 -= jnp.where(first_row, 0.0, pltpu.roll(y_up[1], 1, 0))
            next0 = jnp.where(last_row, 0.0, pltpu.roll(f0, height - 1, 0))
            next1 = jnp.where(last_row, 0.0, pltpu.roll(f1, height - 1, 0))
            b0, b1 = block(low_diag, low_cross, ((1,), (x,)), next0, next1)
            a0 -= b0
            a1 -= b1
            z_up = block(up_diag, up_cross, ((2,), (x,)), f0, f1)
            a0 -= jnp.where(first_lane, 0.0, pltpu.roll(z_up[0], 1, 1))
            a1 -= jnp.where(first_lane, 0.0, pltpu.roll(z_up[1], 1, 1))
            next0 = jnp.where(last_lane, 0.0, pltpu.roll(f0, depth - 1, 1))
            next1 = jnp.where(last_lane, 0.0, pltpu.roll(f1, depth - 1, 1))
            b0, b1 = block(low_diag, low_cross, ((2,), (x,)), next0, next1)
            basis[step, 0, x] = a0 - b0
            basis[step, 1, x] = a1 - b1
        add_dots(step)

        for k in range(2 * REACH + 1):
            if k == REACH:
                continue
            away = k - REACH

            @pl.when((gx + away >= 0) & (gx + away < peers))
            def _():
                well_copy(step, k).wait_recv()

        total = well_send[step]
        for k in range(2 * REACH + 1):
            if k != REACH:
                total += mask[k] * well_recv[step, k]
        if step == 0:
            totals[...] = total
            for r in range(4):
                below = totals[4 + r % 2 : 5 + r % 2]
                denom[r : r + 1] = jnp.where(below > 0.0, below, 1.0)
        means = total[:4] / denom[...]
        for c in range(2):
            mean = jnp.concatenate([means[2 * c : 2 * c + 1], means[2 * c + 1 : 2 * c + 2]], axis=1)
            taken = jnp.concatenate(parts(mean * spread[...], 2), axis=1)
            taken = jnp.dot(taken, layer_twice, preferred_element_type=F32)
            for x in range(width):
                basis[step, c, x] -= taken[x * height : (x + 1) * height]

        halo_copy(step, 2).wait_recv()

        @pl.when(gy == 0)
        def _():
            at = slice(height - 1, height)
            for x in range(width):
                f0, f1 = (y_recv[step, x : x + 1], y_recv[step, width + x : width + x + 1])
                b0, b1 = block(low_diag, low_cross, ((1,), (x, at)), f0, f1)
                basis[step, 0, x, at] -= b0
                basis[step, 1, x, at] -= b1

        @pl.when(gy == 1)
        def _():
            for x in range(width):
                for c in range(2):
                    at = c * width + x
                    basis[step, c, x, 0:1] -= y_recv[step, at : at + 1]

        @pl.when(gx > 0)
        def _():
            halo_copy(step, 0).wait_recv()
            for c in range(2):
                basis[step, c, 0] -= up_recv[step, c]

        @pl.when(gx < peers - 1)
        def _():
            halo_copy(step, 1).wait_recv()
            x = width - 1
            f0, f1 = (down_recv[step, 0], down_recv[step, 1])
            b0, b1 = block(low_diag, low_cross, ((0,), (x,)), f0, f1)
            basis[step, 0, x] -= b0
            basis[step, 1, x] -= b1

    add_dots(POWERS)
    dots[15:16, :] = jnp.zeros((1, depth), F32)

    def dots_copy(index, other):
        return pltpu.make_async_remote_copy(
            src_ref=dots,
            dst_ref=dots_all.at[index],
            send_sem=dots_send_sem.at[index],
            recv_sem=dots_recv_sem.at[index],
            device_id={"gx": other // 2, "gy": other % 2},
            device_id_type=MESH,
        )

    for step in range(1, everyone):
        other = lax.rem(me + step, everyone)
        pltpu.make_async_remote_copy(
            src_ref=dots,
            dst_ref=dots_all.at[me],
            send_sem=dots_send_sem.at[step],
            recv_sem=dots_recv_sem.at[me],
            device_id={"gx": other // 2, "gy": other % 2},
            device_id_type=MESH,
        ).start()
    dots_all[me] = dots[...]
    for step in range(1, everyone):
        other = lax.rem(me + step, everyone)
        dots_copy(other, other).wait_recv()
    gathered = jnp.sum(dots_all[...], axis=0)
    gathered = jnp.broadcast_to(jnp.sum(gathered, axis=1, keepdims=True), gathered.shape)
    gram = {}
    for k in range(POWERS + 1):
        for j in range(k + 1):
            at = k * (k + 1) // 2 + j
            gram[(j, k)] = gathered[at : at + 1, :]
    adjoint, residual = bicgstab_terms(gram)

    for x in range(width):
        fields = []
        for c in range(2):
            values = [vector(k)[c, x] for k in range(POWERS + 1)]
            residual_out[c, x] = combine(residual, values)
            fields.append(combine(adjoint, values))
        f0, f1 = block(spai_diag, spai_cross, ((), (x,)), *fields)
        adjoint_out[0, x] = f0
        adjoint_out[1, x] = f1

    for step in range(POWERS):

        @pl.when(gx < peers - 1)
        def _():
            halo_copy(step, 0).wait_send()

        @pl.when(gx > 0)
        def _():
            halo_copy(step, 1).wait_send()

        halo_copy(step, 2).wait_send()
        for k in range(2 * REACH + 1):
            if k == REACH:
                continue
            away = REACH - k

            @pl.when((gx + away >= 0) & (gx + away < peers))
            def _():
                well_copy(step, k).wait_send()

    for step in range(1, everyone):
        dots_copy(step, me).wait_send()


def shards(peers, *args):
    rhs = args[0]
    _, width, height, depth = rhs.shape
    owned = args[-1].shape[-1]
    buckets = RING * owned
    rows = width * height
    everyone = peers * 2
    plane = (POWERS, 2, height, depth)
    wells = 2 * REACH + 1
    vmem = pl.BlockSpec(memory_space=pltpu.VMEM)
    return pl.pallas_call(
        functools.partial(kernel, peers),
        out_shape=[jax.ShapeDtypeStruct(rhs.shape, F32)] * 2,
        in_specs=[pl.BlockSpec(memory_space=pl.ANY)] * len(args),
        out_specs=[vmem] * 2,
        scratch_shapes=[pltpu.VMEM(a.shape, a.dtype) for a in args]
        + [
            pltpu.SemaphoreType.DMA((len(args),)),
            pltpu.VMEM((POWERS, 2, width, height, depth), F32),
            pltpu.VMEM((POWERS, 2, width, height, depth), F32),
            pltpu.VMEM((2, width, height, depth), F32),
            pltpu.VMEM((rows, buckets), F32),
            pltpu.VMEM((wells, 8, 128), F32),
            pltpu.VMEM((4, 128), F32),
            pltpu.VMEM((8, 128), F32),
            pltpu.VMEM(plane, F32),
            pltpu.VMEM(plane, F32),
            pltpu.VMEM(plane, F32),
            pltpu.VMEM((POWERS, 2 * width, depth), F32),
            pltpu.VMEM((POWERS, 2 * width, depth), F32),
            pltpu.VMEM((POWERS, 8, 128), F32),
            pltpu.VMEM((POWERS, wells, 8, 128), F32),
            pltpu.VMEM((16, depth), F32),
            pltpu.VMEM((everyone, 16, depth), F32),
            pltpu.SemaphoreType.DMA((POWERS, 3)),
            pltpu.SemaphoreType.DMA((POWERS, 3)),
            pltpu.SemaphoreType.DMA((POWERS, wells)),
            pltpu.SemaphoreType.DMA((POWERS, wells)),
            pltpu.SemaphoreType.DMA((everyone,)),
            pltpu.SemaphoreType.DMA((everyone,)),
        ],
        compiler_params=pltpu.CompilerParams(
            collective_id=0, has_side_effects=True, vmem_limit_bytes=60 * 1024 * 1024
        ),
    )(*args)


def solution(mesh):
    cell = P("ens", "gx", "gy", None)
    coupling = P("ens", None, "gx", "gy", None)
    tile = P(("ens", "gx"), "gy", None)
    in_specs = (cell,) * 3 + (coupling,) * 4 + (cell,) * 2 + (tile,) * 5
    return jax.shard_map(
        functools.partial(shards, mesh.shape["gx"]),
        mesh=mesh,
        in_specs=in_specs,
        out_specs=(cell, cell),
        check_vma=False,
    )
```

```python
import functools

import jax
import jax.numpy as jnp
from jax import lax
from jax.experimental import pallas as pl
from jax.experimental.pallas import tpu as pltpu
from jax.sharding import PartitionSpec as P

MESH = pl.DeviceIdType.MESH
ITERS = 2
POWERS = 2 * ITERS
SHIFT = 1.0
RING = 8
REACH = 4
PIECES = 2
F32 = jnp.float32
BF16 = jnp.bfloat16


def parts(value, count):
    pieces = []
    for _ in range(count):
        piece = value.astype(BF16)
        pieces.append(piece)
        value = value - piece.astype(F32)
    return pieces


def rows_dot(first, second):
    return lax.dot_general(first, second, (((1,), (1,)), ((), ())), preferred_element_type=F32)


def combine(terms, vectors):
    total = None
    for term, vector in zip(terms, vectors):
        if term is None:
            continue
        piece = term * vector
        total = piece if total is None else total + piece
    return total


def add(first, second):
    if first is None:
        return second
    if second is None:
        return first
    return first + second


def scale(factor, terms):
    return [None if t is None else factor * t for t in terms]


def plus(first, second):
    return [add(a, b) for a, b in zip(first, second)]


def advance(terms):
    moved = [None] + list(terms[:-1])
    return plus(moved, scale(SHIFT, terms))


def bicgstab_terms(gram):
    def product(first, second):
        total = None
        for i, a in enumerate(first):
            for j, b in enumerate(second):
                if a is not None and b is not None:
                    total = add(total, a * b * gram[(min(i, j), max(i, j))])
        return total

    count = POWERS + 1
    one = jnp.ones_like(gram[(0, 0)])
    shadow = [one] + [None] * (count - 1)
    residual = list(shadow)
    adjoint = [None] * count
    direction = image = None
    rho = alpha = omega = one
    for step in range(ITERS):
        rho_new = product(shadow, residual)
        if step == 0:
            direction = residual
        else:
            beta = rho_new / rho * (alpha / omega)
            direction = plus(residual, scale(beta, plus(direction, scale(-omega, image))))
        image = advance(direction)
        alpha = rho_new / product(shadow, image)
        half = plus(residual, scale(-alpha, image))
        turned = advance(half)
        omega = product(turned, half) / product(turned, turned)
        adjoint = plus(adjoint, plus(scale(alpha, direction), scale(omega, half)))
        residual = plus(half, scale(-omega, turned))
        rho = rho_new
    return adjoint, residual


def kernel(
    peers,
    *refs,
):
    inputs, (adjoint_out, residual_out) = (refs[:14], refs[14:16])
    held, load_sem, refs = (refs[16:30], refs[30], refs[31:])
    run(peers, inputs, held, load_sem, adjoint_out, residual_out, *refs)


def run(
    peers,
    inputs,
    held,
    load_sem,
    adjoint_out,
    residual_out,
    basis,
    lifted,
    diag,
    spread,
    mask,
    denom,
    totals,
    up_send,
    up_recv,
    down_recv,
    y_send,
    y_recv,
    well_send,
    well_recv,
    dots,
    packed,
    dots_all,
    halo_send_sem,
    halo_recv_sem,
    well_send_sem,
    well_recv_sem,
    dots_send_sem,
    dots_recv_sem,
):
    rhs, cell_diag, cell_cross, up_diag, up_cross, low_diag, low_cross = held[:7]
    spai_diag, spai_cross, perf_cell, perf_owner, perf_well, perf_index, storage = held[7:]
    loads = [pltpu.make_async_copy(inputs[k], held[k], load_sem.at[k]) for k in range(14)]
    for k in (0, 7, 8, 9, 10, 11, 12, 13, 3, 4, 1, 2, 5, 6):
        loads[k].start()

    def ready(*which):
        for k in which:
            loads[k].wait()

    gx, gy = lax.axis_index("gx"), lax.axis_index("gy")
    everyone = peers * 2
    me = gx * 2 + gy
    _, width, height, depth = rhs.shape
    rows = width * height
    lanes = perf_cell.shape[-1]
    owned = storage.shape[-1]
    buckets = RING * owned

    well_recv[...] = jnp.zeros_like(well_recv)
    barrier = pltpu.get_barrier_semaphore()
    for step in range(1, everyone):
        other = lax.rem(me + step, everyone)
        pl.semaphore_signal(
            barrier, 1, device_id={"gx": other // 2, "gy": other % 2}, device_id_type=MESH
        )

    lane = lax.broadcasted_iota(jnp.int32, (height, depth), 1)
    row = lax.broadcasted_iota(jnp.int32, (height, depth), 0)
    first_lane, last_lane = (lane == 0, lane == depth - 1)
    first_row, last_row = (row == 0, row == height - 1)

    ready(0, 7, 8)
    pl.semaphore_wait(barrier, everyone - 1)

    def vector(k):
        return rhs if k == 0 else basis.at[k - 1]

    def start_wells(step):
        for k in range(2 * REACH + 1):
            if k == REACH:
                continue
            away = REACH - k

            @pl.when((gx + away >= 0) & (gx + away < peers))
            def _():
                pltpu.make_async_remote_copy(
                    src_ref=well_send.at[step],
                    dst_ref=well_recv.at[step, k],
                    send_sem=well_send_sem.at[step, k],
                    recv_sem=well_recv_sem.at[step, k],
                    device_id={"gx": gx + away},
                    device_id_type=MESH,
                ).start()

    def well_copy(step, k):
        return pltpu.make_async_remote_copy(
            src_ref=well_send.at[step],
            dst_ref=well_recv.at[step, k],
            send_sem=well_send_sem.at[step, k],
            recv_sem=well_recv_sem.at[step, k],
            device_id={"gx": gx},
            device_id_type=MESH,
        )

    def halo_copy(step, kind):
        way, piece = divmod(kind, PIECES)
        at = pl.ds(piece * (height // PIECES), height // PIECES)
        if way == 0:
            src, dst, target = (up_send.at[step, :, at], up_recv.at[step, :, at], {"gx": gx + 1})
        elif way == 1:
            src, dst, target = (
                lifted.at[step, :, 0, at],
                down_recv.at[step, :, at],
                {"gx": gx - 1},
            )
        else:
            src, dst, target = (y_send.at[step], y_recv.at[step], {"gy": 1 - gy})
        return pltpu.make_async_remote_copy(
            src_ref=src,
            dst_ref=dst,
            send_sem=halo_send_sem.at[step, kind],
            recv_sem=halo_recv_sem.at[step, kind],
            device_id=target,
            device_id_type=MESH,
        )

    def block(diag_ref, cross_ref, at, f0, f1):
        d0, d1 = (diag_ref[(*at[0], 0, *at[1])], diag_ref[(*at[0], 1, *at[1])])
        c0, c1 = (cross_ref[(*at[0], 0, *at[1])], cross_ref[(*at[0], 1, *at[1])])
        return (d0 * f0 + c1 * f1, c0 * f0 + d1 * f1)

    def add_dots(k):
        sums = [jnp.zeros((8, depth), F32) for _ in range(k + 1)]
        for c in range(2):
            for x in range(width):
                last = vector(k)[c, x]
                for j in range(k + 1):
                    other = last if j == k else vector(j)[c, x]
                    sums[j] += jnp.sum((last * other).reshape(height // 8, 8, depth), axis=0)
        for j in range(k + 1):
            at = k * (k + 1) // 2 + j
            dots[at : at + 1, :] = jnp.sum(sums[j], axis=0, keepdims=True)

    def lift(step, x, at):
        source = vector(step)
        f0, f1 = block(spai_diag, spai_cross, ((), (x, at)), source[0, x, at], source[1, x, at])
        lifted[step, 0, x, at] = f0
        lifted[step, 1, x, at] = f1
        return f0, f1

    def start_planes(step, piece):
        @pl.when(gx > 0)
        def _():
            halo_copy(step, PIECES + piece).start()

        @pl.when(gx < peers - 1)
        def _():
            halo_copy(step, piece).start()

    def send_planes(step, piece):
        at = slice(piece * (height // PIECES), (piece + 1) * (height // PIECES))
        lift(step, 0, at)
        f0, f1 = lift(step, width - 1, at)
        if step == 0 and piece == 0:
            ready(3, 4)
        p0, p1 = block(up_diag, up_cross, ((0,), (width - 1, at)), f0, f1)
        up_send[step, 0, at] = p0
        up_send[step, 1, at] = p1
        if piece == 0:
            start_planes(step, piece)

    for piece in range(PIECES):
        send_planes(0, piece)

    ready(9, 10, 11, 12, 13)
    cells = perf_cell[0]
    bucket_of = (perf_owner[0] & (RING - 1)) * owned + perf_well[0]
    row_of, layer_of = (cells // depth, cells % depth)
    weights = perf_index[0]
    in_row = lax.broadcasted_iota(jnp.int32, (rows, lanes), 0) == row_of
    in_bucket = lax.broadcasted_iota(jnp.int32, (buckets, lanes), 0) == bucket_of
    in_layer = lax.broadcasted_iota(jnp.int32, (depth, lanes), 0) == layer_of
    hot_row = in_row.astype(F32).astype(BF16)
    hot_bucket = in_bucket.astype(F32).astype(BF16)
    hot_layer = in_layer.astype(F32).astype(BF16)
    spread_now = jnp.zeros((rows, buckets), F32)
    extra = jnp.zeros((rows, depth), F32)
    for piece in parts(weights, 3):
        piece = piece.astype(F32)
        spread_now += rows_dot(hot_row, jnp.where(in_bucket, piece, 0.0).astype(BF16))
        extra += rows_dot(hot_row, jnp.where(in_layer, piece, 0.0).astype(BF16))
    spread[...] = spread_now
    layer_of_bucket = jnp.minimum(rows_dot(hot_bucket, hot_layer), 1.0).astype(BF16)
    bucket_of_layer = jnp.minimum(rows_dot(hot_layer, hot_bucket), 1.0).astype(BF16)
    layer_twice = jnp.concatenate([layer_of_bucket, layer_of_bucket], axis=0)
    bucket_twice = jnp.concatenate([bucket_of_layer, bucket_of_layer], axis=0)
    ready(1)
    for c in range(2):
        for x in range(width):
            diag[c, x] = cell_diag[c, x] + extra[x * height : (x + 1) * height]

    place = lax.broadcasted_iota(jnp.int32, (owned, buckets), 1)
    slot = lax.broadcasted_iota(jnp.int32, (owned, buckets), 0)
    mine = (place // owned == (gx & (RING - 1))) & (place % owned == slot)
    stored = jnp.zeros((8, buckets), F32)
    for piece in parts(jnp.broadcast_to(storage[0], (8, owned)), 3):
        stored += jnp.dot(piece, mine.astype(F32).astype(BF16), preferred_element_type=F32)
    weight_sums = jnp.sum(spread_now, axis=0, keepdims=True) + stored[:1]

    tile_row = lax.broadcasted_iota(jnp.int32, (8, 128), 0)
    tile_lane = lax.broadcasted_iota(jnp.int32, (8, 128), 1)
    residue = ((tile_row % 2) * 128 + tile_lane) // owned
    here = (residue - gx + 2) & (RING - 1)
    for k in range(2 * REACH + 1):
        away = k - REACH
        there = (residue - gx - away + 2) & (RING - 1)
        same = (here < 5) & (there < 5) & (here == there + away)
        mask[k] = same.astype(F32)

    for step in range(POWERS):
        source = vector(step)
        for x in range(1, width - 1):
            lift(step, x, slice(0, height))

        @pl.when(gy == 0)
        def _():
            at = slice(height - 1, height)
            for x in range(width):
                p0, p1 = block(
                    up_diag,
                    up_cross,
                    ((1,), (x, at)),
                    lifted[step, 0, x, at],
                    lifted[step, 1, x, at],
                )
                y_send[step, x : x + 1] = p0
                y_send[step, width + x : width + x + 1] = p1

        @pl.when(gy == 1)
        def _():
            for x in range(width):
                for c in range(2):
                    y_send[step, c * width + x : c * width + x + 1] = lifted[step, c, x, 0:1]

        halo_copy(step, 2 * PIECES).start()

        for c in range(2):
            field = lifted[step, c].reshape(rows, depth)
            picked = jnp.dot(
                jnp.concatenate(parts(field, 2), axis=1),
                bucket_twice,
                preferred_element_type=F32,
            )
            sums = jnp.sum(picked * spread[...], axis=0, keepdims=True)
            well_send[step, 2 * c : 2 * c + 1] = sums[:, :128]
            well_send[step, 2 * c + 1 : 2 * c + 2] = sums[:, 128:]
        well_send[step, 4:5] = weight_sums[:, :128]
        well_send[step, 5:6] = weight_sums[:, 128:]
        well_send[step, 6:8] = jnp.zeros((2, 128), F32)
        start_wells(step)
        for piece in range(1, PIECES):
            start_planes(step, piece)

        if step == 0:
            ready(2, 5, 6)
        carry = None
        for x in range(width):
            f0, f1 = (lifted[step, 0, x], lifted[step, 1, x])
            here = ((), (x,))
            a0, a1 = block(diag, cell_cross, here, f0, f1)
            a0 -= SHIFT * source[0, x]
            a1 -= SHIFT * source[1, x]
            if carry is not None:
                a0 -= carry[0]
                a1 -= carry[1]
            if x < width - 1:
                carry = block(up_diag, up_cross, ((0,), (x,)), f0, f1)
                b0, b1 = block(
                    low_diag, low_cross, ((0,), (x,)), lifted[step, 0, x + 1], lifted[step, 1, x + 1]
                )
                a0 -= b0
                a1 -= b1
            y_up = block(up_diag, up_cross, ((1,), (x,)), f0, f1)
            a0 -= jnp.where(first_row, 0.0, pltpu.roll(y_up[0], 1, 0))
            a1 -= jnp.where(first_row, 0.0, pltpu.roll(y_up[1], 1, 0))
            next0 = jnp.where(last_row, 0.0, pltpu.roll(f0, height - 1, 0))
            next1 = jnp.where(last_row, 0.0, pltpu.roll(f1, height - 1, 0))
            b0, b1 = block(low_diag, low_cross, ((1,), (x,)), next0, next1)
            a0 -= b0
            a1 -= b1
            z_up = block(up_diag, up_cross, ((2,), (x,)), f0, f1)
            a0 -= jnp.where(first_lane, 0.0, pltpu.roll(z_up[0], 1, 1))
            a1 -= jnp.where(first_lane, 0.0, pltpu.roll(z_up[1], 1, 1))
            next0 = jnp.where(last_lane, 0.0, pltpu.roll(f0, depth - 1, 1))
            next1 = jnp.where(last_lane, 0.0, pltpu.roll(f1, depth - 1, 1))
            b0, b1 = block(low_diag, low_cross, ((2,), (x,)), next0, next1)
            basis[step, 0, x] = a0 - b0
            basis[step, 1, x] = a1 - b1
        add_dots(step)

        for k in range(2 * REACH + 1):
            if k == REACH:
                continue
            away = k - REACH

            @pl.when((gx + away >= 0) & (gx + away < peers))
            def _():
                well_copy(step, k).wait_recv()

        total = well_send[step]
        for k in range(2 * REACH + 1):
            if k != REACH:
                total += mask[k] * well_recv[step, k]
        if step == 0:
            totals[...] = total
            for r in range(4):
                below = totals[4 + r % 2 : 5 + r % 2]
                denom[r : r + 1] = jnp.where(below > 0.0, below, 1.0)
        means = total[:4] / denom[...]
        for c in range(2):
            mean = jnp.concatenate([means[2 * c : 2 * c + 1], means[2 * c + 1 : 2 * c + 2]], axis=1)
            taken = jnp.concatenate(parts(mean * spread[...], 2), axis=1)
            taken = jnp.dot(taken, layer_twice, preferred_element_type=F32)
            for x in range(width):
                basis[step, c, x] -= taken[x * height : (x + 1) * height]

        halo_copy(step, 2 * PIECES).wait_recv()

        @pl.when(gy == 0)
        def _():
            at = slice(height - 1, height)
            for x in range(width):
                f0, f1 = (y_recv[step, x : x + 1], y_recv[step, width + x : width + x + 1])
                b0, b1 = block(low_diag, low_cross, ((1,), (x, at)), f0, f1)
                basis[step, 0, x, at] -= b0
                basis[step, 1, x, at] -= b1

        @pl.when(gy == 1)
        def _():
            for x in range(width):
                for c in range(2):
                    at = c * width + x
                    basis[step, c, x, 0:1] -= y_recv[step, at : at + 1]

        for piece in range(PIECES):
            at = slice(piece * (height // PIECES), (piece + 1) * (height // PIECES))

            @pl.when(gx > 0)
            def _():
                halo_copy(step, piece).wait_recv()
                for c in range(2):
                    basis[step, c, 0, at] -= up_recv[step, c, at]

            @pl.when(gx < peers - 1)
            def _():
                halo_copy(step, PIECES + piece).wait_recv()
                x = width - 1
                f0, f1 = (down_recv[step, 0, at], down_recv[step, 1, at])
                b0, b1 = block(low_diag, low_cross, ((0,), (x, at)), f0, f1)
                basis[step, 0, x, at] -= b0
                basis[step, 1, x, at] -= b1

            if step < POWERS - 1:
                send_planes(step + 1, piece)

    add_dots(POWERS)
    dots[15:16, :] = jnp.zeros((1, depth), F32)
    on_lane = lax.broadcasted_iota(jnp.int32, (16, depth), 1)
    on_lane = on_lane == lax.broadcasted_iota(jnp.int32, (16, depth), 0)
    sums = jnp.sum(dots[...], axis=1, keepdims=True)
    packed[...] = jnp.sum(jnp.where(on_lane, sums, 0.0), axis=0, keepdims=True)

    def dots_copy(index, other):
        return pltpu.make_async_remote_copy(
            src_ref=packed,
            dst_ref=dots_all.at[index],
            send_sem=dots_send_sem.at[index],
            recv_sem=dots_recv_sem.at[index],
            device_id={"gx": other // 2, "gy": other % 2},
            device_id_type=MESH,
        )

    for step in range(1, everyone):
        other = lax.rem(me + step, everyone)
        pltpu.make_async_remote_copy(
            src_ref=packed,
            dst_ref=dots_all.at[me],
            send_sem=dots_send_sem.at[step],
            recv_sem=dots_recv_sem.at[me],
            device_id={"gx": other // 2, "gy": other % 2},
            device_id_type=MESH,
        ).start()
    dots_all[me] = packed[...]
    for step in range(1, everyone):
        other = lax.rem(me + step, everyone)
        dots_copy(other, other).wait_recv()
    gathered = jnp.where(on_lane, jnp.sum(dots_all[...], axis=0), 0.0)
    gathered = jnp.broadcast_to(jnp.sum(gathered, axis=1, keepdims=True), gathered.shape)
    gram = {}
    for k in range(POWERS + 1):
        for j in range(k + 1):
            at = k * (k + 1) // 2 + j
            gram[(j, k)] = gathered[at : at + 1, :]
    adjoint, residual = bicgstab_terms(gram)

    for x in range(width):
        fields = []
        for c in range(2):
            values = [vector(k)[c, x] for k in range(POWERS + 1)]
            residual_out[c, x] = combine(residual, values)
            fields.append(combine(adjoint, values))
        f0, f1 = block(spai_diag, spai_cross, ((), (x,)), *fields)
        adjoint_out[0, x] = f0
        adjoint_out[1, x] = f1

    for step in range(POWERS):

        for piece in range(PIECES):

            @pl.when(gx < peers - 1)
            def _():
                halo_copy(step, piece).wait_send()

            @pl.when(gx > 0)
            def _():
                halo_copy(step, PIECES + piece).wait_send()

        halo_copy(step, 2 * PIECES).wait_send()
        for k in range(2 * REACH + 1):
            if k == REACH:
                continue
            away = REACH - k

            @pl.when((gx + away >= 0) & (gx + away < peers))
            def _():
                well_copy(step, k).wait_send()

    for step in range(1, everyone):
        dots_copy(step, me).wait_send()


def store(first, second, first_out, second_out, sem):
    copies = [
        pltpu.make_async_copy(first, first_out, sem.at[0]),
        pltpu.make_async_copy(second, second_out, sem.at[1]),
    ]
    for copy in copies:
        copy.start()
    for copy in copies:
        copy.wait()


def shards(peers, *args):
    rhs = args[0]
    _, width, height, depth = rhs.shape
    owned = args[-1].shape[-1]
    buckets = RING * owned
    rows = width * height
    everyone = peers * 2
    plane = (POWERS, 2, height, depth)
    wells = 2 * REACH + 1
    vmem = pl.BlockSpec(memory_space=pltpu.VMEM)
    results = pl.pallas_call(
        functools.partial(kernel, peers),
        out_shape=[jax.ShapeDtypeStruct(rhs.shape, F32)] * 2,
        in_specs=[pl.BlockSpec(memory_space=pl.ANY)] * len(args),
        out_specs=[vmem] * 2,
        scratch_shapes=[pltpu.VMEM(a.shape, a.dtype) for a in args]
        + [
            pltpu.SemaphoreType.DMA((len(args),)),
            pltpu.VMEM((POWERS, 2, width, height, depth), F32),
            pltpu.VMEM((POWERS, 2, width, height, depth), F32),
            pltpu.VMEM((2, width, height, depth), F32),
            pltpu.VMEM((rows, buckets), F32),
            pltpu.VMEM((wells, 8, 128), F32),
            pltpu.VMEM((4, 128), F32),
            pltpu.VMEM((8, 128), F32),
            pltpu.VMEM(plane, F32),
            pltpu.VMEM(plane, F32),
            pltpu.VMEM(plane, F32),
            pltpu.VMEM((POWERS, 2 * width, depth), F32),
            pltpu.VMEM((POWERS, 2 * width, depth), F32),
            pltpu.VMEM((POWERS, 8, 128), F32),
            pltpu.VMEM((POWERS, wells, 8, 128), F32),
            pltpu.VMEM((16, depth), F32),
            pltpu.VMEM((1, depth), F32),
            pltpu.VMEM((everyone, 1, depth), F32),
            pltpu.SemaphoreType.DMA((POWERS, 2 * PIECES + 1)),
            pltpu.SemaphoreType.DMA((POWERS, 2 * PIECES + 1)),
            pltpu.SemaphoreType.DMA((POWERS, wells)),
            pltpu.SemaphoreType.DMA((POWERS, wells)),
            pltpu.SemaphoreType.DMA((everyone,)),
            pltpu.SemaphoreType.DMA((everyone,)),
        ],
        compiler_params=pltpu.CompilerParams(
            collective_id=0, has_side_effects=True, vmem_limit_bytes=60 * 1024 * 1024
        ),
    )(*args)
    anywhere = pl.BlockSpec(memory_space=pl.ANY)
    return pl.pallas_call(
        store,
        out_shape=[jax.ShapeDtypeStruct(rhs.shape, F32)] * 2,
        in_specs=[vmem] * 2,
        out_specs=[anywhere] * 2,
        scratch_shapes=[pltpu.SemaphoreType.DMA((2,))],
    )(*results)


def solution(mesh):
    cell = P("ens", "gx", "gy", None)
    coupling = P("ens", None, "gx", "gy", None)
    tile = P(("ens", "gx"), "gy", None)
    in_specs = (cell,) * 3 + (coupling,) * 4 + (cell,) * 2 + (tile,) * 5
    return jax.shard_map(
        functools.partial(shards, mesh.shape["gx"]),
        mesh=mesh,
        in_specs=in_specs,
        out_specs=(cell, cell),
        check_vma=False,
    )
```

```python
import functools

import jax
import jax.numpy as jnp
from jax import lax
from jax.experimental import pallas as pl
from jax.experimental.pallas import tpu as pltpu
from jax.sharding import PartitionSpec as P

MESH = pl.DeviceIdType.MESH
ITERS = 2
POWERS = 2 * ITERS
SHIFT = 1.0
RING = 8
REACH = 4
PIECES = 2
F32 = jnp.float32
BF16 = jnp.bfloat16


def parts(value, count):
    pieces = []
    for _ in range(count):
        piece = value.astype(BF16)
        pieces.append(piece)
        value = value - piece.astype(F32)
    return pieces


def rows_dot(first, second):
    return lax.dot_general(first, second, (((1,), (1,)), ((), ())), preferred_element_type=F32)


def combine(terms, vectors):
    total = None
    for term, vector in zip(terms, vectors):
        if term is None:
            continue
        piece = term * vector
        total = piece if total is None else total + piece
    return total


def add(first, second):
    if first is None:
        return second
    if second is None:
        return first
    return first + second


def scale(factor, terms):
    return [None if t is None else factor * t for t in terms]


def plus(first, second):
    return [add(a, b) for a, b in zip(first, second)]


def advance(terms):
    moved = [None] + list(terms[:-1])
    return plus(moved, scale(SHIFT, terms))


def bicgstab_terms(gram):
    def product(first, second):
        total = None
        for i, a in enumerate(first):
            for j, b in enumerate(second):
                if a is not None and b is not None:
                    total = add(total, a * b * gram[(min(i, j), max(i, j))])
        return total

    count = POWERS + 1
    one = jnp.ones_like(gram[(0, 0)])
    shadow = [one] + [None] * (count - 1)
    residual = list(shadow)
    adjoint = [None] * count
    direction = image = None
    rho = alpha = omega = one
    for step in range(ITERS):
        rho_new = product(shadow, residual)
        if step == 0:
            direction = residual
        else:
            beta = rho_new / rho * (alpha / omega)
            direction = plus(residual, scale(beta, plus(direction, scale(-omega, image))))
        image = advance(direction)
        alpha = rho_new / product(shadow, image)
        half = plus(residual, scale(-alpha, image))
        turned = advance(half)
        omega = product(turned, half) / product(turned, turned)
        adjoint = plus(adjoint, plus(scale(alpha, direction), scale(omega, half)))
        residual = plus(half, scale(-omega, turned))
        rho = rho_new
    return adjoint, residual


def kernel(
    peers,
    *refs,
):
    inputs, (adjoint_out, residual_out) = (refs[:14], refs[14:16])
    held, load_sem, refs = (refs[16:30], refs[30], refs[31:])
    run(peers, inputs, held, load_sem, adjoint_out, residual_out, *refs)


def run(
    peers,
    inputs,
    held,
    load_sem,
    adjoint_out,
    residual_out,
    basis,
    lifted,
    diag,
    spread,
    mask,
    denom,
    totals,
    up_send,
    up_recv,
    down_recv,
    y_send,
    y_recv,
    well_send,
    well_recv,
    dots,
    packed,
    dots_all,
    halo_send_sem,
    halo_recv_sem,
    well_send_sem,
    well_recv_sem,
    dots_send_sem,
    dots_recv_sem,
):
    rhs, cell_diag, cell_cross, up_diag, up_cross, low_diag, low_cross = held[:7]
    spai_diag, spai_cross, perf_cell, perf_owner, perf_well, perf_index, storage = held[7:]
    loads = [pltpu.make_async_copy(inputs[k], held[k], load_sem.at[k]) for k in range(14)]
    for k in (0, 7, 8, 9, 10, 11, 12, 13, 3, 4, 1, 2, 5, 6):
        loads[k].start()

    def ready(*which):
        for k in which:
            loads[k].wait()

    gx, gy = lax.axis_index("gx"), lax.axis_index("gy")
    everyone = peers * 2
    me = gx * 2 + gy
    _, width, height, depth = rhs.shape
    rows = width * height
    lanes = perf_cell.shape[-1]
    owned = storage.shape[-1]
    buckets = RING * owned

    well_recv[...] = jnp.zeros_like(well_recv)
    barrier = pltpu.get_barrier_semaphore()
    chained = REACH <= peers <= 2 * REACH
    if chained:
        pl.semaphore_signal(barrier, 1, device_id={"gy": 1 - gy}, device_id_type=MESH)
        for away in range(-REACH, REACH + 1):
            if away == 0:
                continue

            @pl.when((gx + away >= 0) & (gx + away < peers))
            def _():
                pl.semaphore_signal(barrier, 1, device_id={"gx": gx + away}, device_id_type=MESH)

    else:
        for step in range(1, everyone):
            other = lax.rem(me + step, everyone)
            pl.semaphore_signal(
                barrier, 1, device_id={"gx": other // 2, "gy": other % 2}, device_id_type=MESH
            )

    lane = lax.broadcasted_iota(jnp.int32, (height, depth), 1)
    row = lax.broadcasted_iota(jnp.int32, (height, depth), 0)
    first_lane, last_lane = (lane == 0, lane == depth - 1)
    first_row, last_row = (row == 0, row == height - 1)

    ready(0, 7, 8)
    if chained:
        near = 1
        for away in range(1, REACH + 1):
            near = near + (gx + peers - away) // peers + 1 - (gx + away) // peers
        pl.semaphore_wait(barrier, near)
    else:
        pl.semaphore_wait(barrier, everyone - 1)

    def vector(k):
        return rhs if k == 0 else basis.at[k - 1]

    def start_wells(step):
        for k in range(2 * REACH + 1):
            if k == REACH:
                continue
            away = REACH - k

            @pl.when((gx + away >= 0) & (gx + away < peers))
            def _():
                pltpu.make_async_remote_copy(
                    src_ref=well_send.at[step],
                    dst_ref=well_recv.at[step, k],
                    send_sem=well_send_sem.at[step, k],
                    recv_sem=well_recv_sem.at[step, k],
                    device_id={"gx": gx + away},
                    device_id_type=MESH,
                ).start()

    def well_copy(step, k):
        return pltpu.make_async_remote_copy(
            src_ref=well_send.at[step],
            dst_ref=well_recv.at[step, k],
            send_sem=well_send_sem.at[step, k],
            recv_sem=well_recv_sem.at[step, k],
            device_id={"gx": gx},
            device_id_type=MESH,
        )

    def halo_copy(step, kind):
        way, piece = divmod(kind, PIECES)
        at = pl.ds(piece * (height // PIECES), height // PIECES)
        if way == 0:
            src, dst, target = (up_send.at[step, :, at], up_recv.at[step, :, at], {"gx": gx + 1})
        elif way == 1:
            src, dst, target = (
                lifted.at[step, :, 0, at],
                down_recv.at[step, :, at],
                {"gx": gx - 1},
            )
        else:
            src, dst, target = (y_send.at[step], y_recv.at[step], {"gy": 1 - gy})
        return pltpu.make_async_remote_copy(
            src_ref=src,
            dst_ref=dst,
            send_sem=halo_send_sem.at[step, kind],
            recv_sem=halo_recv_sem.at[step, kind],
            device_id=target,
            device_id_type=MESH,
        )

    def block(diag_ref, cross_ref, at, f0, f1):
        d0, d1 = (diag_ref[(*at[0], 0, *at[1])], diag_ref[(*at[0], 1, *at[1])])
        c0, c1 = (cross_ref[(*at[0], 0, *at[1])], cross_ref[(*at[0], 1, *at[1])])
        return (d0 * f0 + c1 * f1, c0 * f0 + d1 * f1)

    def add_dots(k):
        sums = [jnp.zeros((8, depth), F32) for _ in range(k + 1)]
        for c in range(2):
            for x in range(width):
                last = vector(k)[c, x]
                for j in range(k + 1):
                    other = last if j == k else vector(j)[c, x]
                    sums[j] += jnp.sum((last * other).reshape(height // 8, 8, depth), axis=0)
        for j in range(k + 1):
            at = k * (k + 1) // 2 + j
            dots[at : at + 1, :] = jnp.sum(sums[j], axis=0, keepdims=True)

    def lift(step, x, at):
        source = vector(step)
        f0, f1 = block(spai_diag, spai_cross, ((), (x, at)), source[0, x, at], source[1, x, at])
        lifted[step, 0, x, at] = f0
        lifted[step, 1, x, at] = f1
        return f0, f1

    def start_planes(step, piece):
        @pl.when(gx > 0)
        def _():
            halo_copy(step, PIECES + piece).start()

        @pl.when(gx < peers - 1)
        def _():
            halo_copy(step, piece).start()

    def send_planes(step, piece):
        at = slice(piece * (height // PIECES), (piece + 1) * (height // PIECES))
        lift(step, 0, at)
        f0, f1 = lift(step, width - 1, at)
        if step == 0 and piece == 0:
            ready(3, 4)
        p0, p1 = block(up_diag, up_cross, ((0,), (width - 1, at)), f0, f1)
        up_send[step, 0, at] = p0
        up_send[step, 1, at] = p1
        if piece == 0:
            start_planes(step, piece)

    for piece in range(PIECES):
        send_planes(0, piece)

    ready(9, 10, 11, 12, 13)
    cells = perf_cell[0]
    bucket_of = (perf_owner[0] & (RING - 1)) * owned + perf_well[0]
    row_of, layer_of = (cells // depth, cells % depth)
    weights = perf_index[0]
    in_row = lax.broadcasted_iota(jnp.int32, (rows, lanes), 0) == row_of
    in_bucket = lax.broadcasted_iota(jnp.int32, (buckets, lanes), 0) == bucket_of
    in_layer = lax.broadcasted_iota(jnp.int32, (depth, lanes), 0) == layer_of
    hot_row = in_row.astype(F32).astype(BF16)
    hot_bucket = in_bucket.astype(F32).astype(BF16)
    hot_layer = in_layer.astype(F32).astype(BF16)
    spread_now = jnp.zeros((rows, buckets), F32)
    extra = jnp.zeros((rows, depth), F32)
    for piece in parts(weights, 3):
        piece = piece.astype(F32)
        spread_now += rows_dot(hot_row, jnp.where(in_bucket, piece, 0.0).astype(BF16))
        extra += rows_dot(hot_row, jnp.where(in_layer, piece, 0.0).astype(BF16))
    spread[...] = spread_now
    layer_of_bucket = jnp.minimum(rows_dot(hot_bucket, hot_layer), 1.0).astype(BF16)
    bucket_of_layer = jnp.minimum(rows_dot(hot_layer, hot_bucket), 1.0).astype(BF16)
    layer_twice = jnp.concatenate([layer_of_bucket, layer_of_bucket], axis=0)
    bucket_twice = jnp.concatenate([bucket_of_layer, bucket_of_layer], axis=0)
    ready(1)
    for c in range(2):
        for x in range(width):
            diag[c, x] = cell_diag[c, x] + extra[x * height : (x + 1) * height]

    place = lax.broadcasted_iota(jnp.int32, (owned, buckets), 1)
    slot = lax.broadcasted_iota(jnp.int32, (owned, buckets), 0)
    mine = (place // owned == (gx & (RING - 1))) & (place % owned == slot)
    stored = jnp.zeros((8, buckets), F32)
    for piece in parts(jnp.broadcast_to(storage[0], (8, owned)), 3):
        stored += jnp.dot(piece, mine.astype(F32).astype(BF16), preferred_element_type=F32)
    weight_sums = jnp.sum(spread_now, axis=0, keepdims=True) + stored[:1]

    tile_row = lax.broadcasted_iota(jnp.int32, (8, 128), 0)
    tile_lane = lax.broadcasted_iota(jnp.int32, (8, 128), 1)
    residue = ((tile_row % 2) * 128 + tile_lane) // owned
    here = (residue - gx + 2) & (RING - 1)
    for k in range(2 * REACH + 1):
        away = k - REACH
        there = (residue - gx - away + 2) & (RING - 1)
        same = (here < 5) & (there < 5) & (here == there + away)
        mask[k] = same.astype(F32)

    for step in range(POWERS):
        source = vector(step)
        for x in range(1, width - 1):
            lift(step, x, slice(0, height))

        @pl.when(gy == 0)
        def _():
            at = slice(height - 1, height)
            for x in range(width):
                p0, p1 = block(
                    up_diag,
                    up_cross,
                    ((1,), (x, at)),
                    lifted[step, 0, x, at],
                    lifted[step, 1, x, at],
                )
                y_send[step, x : x + 1] = p0
                y_send[step, width + x : width + x + 1] = p1

        @pl.when(gy == 1)
        def _():
            for x in range(width):
                for c in range(2):
                    y_send[step, c * width + x : c * width + x + 1] = lifted[step, c, x, 0:1]

        halo_copy(step, 2 * PIECES).start()

        for c in range(2):
            field = lifted[step, c].reshape(rows, depth)
            picked = jnp.dot(
                jnp.concatenate(parts(field, 2), axis=1),
                bucket_twice,
                preferred_element_type=F32,
            )
            sums = jnp.sum(picked * spread[...], axis=0, keepdims=True)
            well_send[step, 2 * c : 2 * c + 1] = sums[:, :128]
            well_send[step, 2 * c + 1 : 2 * c + 2] = sums[:, 128:]
        well_send[step, 4:5] = weight_sums[:, :128]
        well_send[step, 5:6] = weight_sums[:, 128:]
        well_send[step, 6:8] = jnp.zeros((2, 128), F32)
        start_wells(step)
        for piece in range(1, PIECES):
            start_planes(step, piece)

        if step == 0:
            ready(2, 5, 6)
        carry = None
        for x in range(width):
            f0, f1 = (lifted[step, 0, x], lifted[step, 1, x])
            here = ((), (x,))
            a0, a1 = block(diag, cell_cross, here, f0, f1)
            a0 -= SHIFT * source[0, x]
            a1 -= SHIFT * source[1, x]
            if carry is not None:
                a0 -= carry[0]
                a1 -= carry[1]
            if x < width - 1:
                carry = block(up_diag, up_cross, ((0,), (x,)), f0, f1)
                b0, b1 = block(
                    low_diag, low_cross, ((0,), (x,)), lifted[step, 0, x + 1], lifted[step, 1, x + 1]
                )
                a0 -= b0
                a1 -= b1
            y_up = block(up_diag, up_cross, ((1,), (x,)), f0, f1)
            a0 -= jnp.where(first_row, 0.0, pltpu.roll(y_up[0], 1, 0))
            a1 -= jnp.where(first_row, 0.0, pltpu.roll(y_up[1], 1, 0))
            next0 = jnp.where(last_row, 0.0, pltpu.roll(f0, height - 1, 0))
            next1 = jnp.where(last_row, 0.0, pltpu.roll(f1, height - 1, 0))
            b0, b1 = block(low_diag, low_cross, ((1,), (x,)), next0, next1)
            a0 -= b0
            a1 -= b1
            z_up = block(up_diag, up_cross, ((2,), (x,)), f0, f1)
            a0 -= jnp.where(first_lane, 0.0, pltpu.roll(z_up[0], 1, 1))
            a1 -= jnp.where(first_lane, 0.0, pltpu.roll(z_up[1], 1, 1))
            next0 = jnp.where(last_lane, 0.0, pltpu.roll(f0, depth - 1, 1))
            next1 = jnp.where(last_lane, 0.0, pltpu.roll(f1, depth - 1, 1))
            b0, b1 = block(low_diag, low_cross, ((2,), (x,)), next0, next1)
            basis[step, 0, x] = a0 - b0
            basis[step, 1, x] = a1 - b1
        add_dots(step)

        for k in range(2 * REACH + 1):
            if k == REACH:
                continue
            away = k - REACH

            @pl.when((gx + away >= 0) & (gx + away < peers))
            def _():
                well_copy(step, k).wait_recv()

        total = well_send[step]
        for k in range(2 * REACH + 1):
            if k != REACH:
                total += mask[k] * well_recv[step, k]
        if step == 0:
            totals[...] = total
            for r in range(4):
                below = totals[4 + r % 2 : 5 + r % 2]
                denom[r : r + 1] = jnp.where(below > 0.0, below, 1.0)
        means = total[:4] / denom[...]
        for c in range(2):
            mean = jnp.concatenate([means[2 * c : 2 * c + 1], means[2 * c + 1 : 2 * c + 2]], axis=1)
            taken = jnp.concatenate(parts(mean * spread[...], 2), axis=1)
            taken = jnp.dot(taken, layer_twice, preferred_element_type=F32)
            for x in range(width):
                basis[step, c, x] -= taken[x * height : (x + 1) * height]

        halo_copy(step, 2 * PIECES).wait_recv()

        @pl.when(gy == 0)
        def _():
            at = slice(height - 1, height)
            for x in range(width):
                f0, f1 = (y_recv[step, x : x + 1], y_recv[step, width + x : width + x + 1])
                b0, b1 = block(low_diag, low_cross, ((1,), (x, at)), f0, f1)
                basis[step, 0, x, at] -= b0
                basis[step, 1, x, at] -= b1

        @pl.when(gy == 1)
        def _():
            for x in range(width):
                for c in range(2):
                    at = c * width + x
                    basis[step, c, x, 0:1] -= y_recv[step, at : at + 1]

        for piece in range(PIECES):
            at = slice(piece * (height // PIECES), (piece + 1) * (height // PIECES))

            @pl.when(gx > 0)
            def _():
                halo_copy(step, piece).wait_recv()
                for c in range(2):
                    basis[step, c, 0, at] -= up_recv[step, c, at]

            @pl.when(gx < peers - 1)
            def _():
                halo_copy(step, PIECES + piece).wait_recv()
                x = width - 1
                f0, f1 = (down_recv[step, 0, at], down_recv[step, 1, at])
                b0, b1 = block(low_diag, low_cross, ((0,), (x, at)), f0, f1)
                basis[step, 0, x, at] -= b0
                basis[step, 1, x, at] -= b1

            if step < POWERS - 1:
                send_planes(step + 1, piece)

    add_dots(POWERS)
    dots[15:16, :] = jnp.zeros((1, depth), F32)
    on_lane = lax.broadcasted_iota(jnp.int32, (16, depth), 1)
    on_lane = on_lane == lax.broadcasted_iota(jnp.int32, (16, depth), 0)
    sums = jnp.sum(dots[...], axis=1, keepdims=True)
    packed[...] = jnp.sum(jnp.where(on_lane, sums, 0.0), axis=0, keepdims=True)

    def dots_copy(index, other):
        return pltpu.make_async_remote_copy(
            src_ref=packed,
            dst_ref=dots_all.at[index],
            send_sem=dots_send_sem.at[index],
            recv_sem=dots_recv_sem.at[index],
            device_id={"gx": other // 2, "gy": other % 2},
            device_id_type=MESH,
        )

    for step in range(1, everyone):
        other = lax.rem(me + step, everyone)
        pltpu.make_async_remote_copy(
            src_ref=packed,
            dst_ref=dots_all.at[me],
            send_sem=dots_send_sem.at[step],
            recv_sem=dots_recv_sem.at[me],
            device_id={"gx": other // 2, "gy": other % 2},
            device_id_type=MESH,
        ).start()
    dots_all[me] = packed[...]
    for step in range(1, everyone):
        other = lax.rem(me + step, everyone)
        dots_copy(other, other).wait_recv()
    gathered = jnp.where(on_lane, jnp.sum(dots_all[...], axis=0), 0.0)
    gathered = jnp.broadcast_to(jnp.sum(gathered, axis=1, keepdims=True), gathered.shape)
    gram = {}
    for k in range(POWERS + 1):
        for j in range(k + 1):
            at = k * (k + 1) // 2 + j
            gram[(j, k)] = gathered[at : at + 1, :]
    adjoint, residual = bicgstab_terms(gram)

    for x in range(width):
        fields = []
        for c in range(2):
            values = [vector(k)[c, x] for k in range(POWERS + 1)]
            residual_out[c, x] = combine(residual, values)
            fields.append(combine(adjoint, values))
        f0, f1 = block(spai_diag, spai_cross, ((), (x,)), *fields)
        adjoint_out[0, x] = f0
        adjoint_out[1, x] = f1

    for step in range(POWERS):

        for piece in range(PIECES):

            @pl.when(gx < peers - 1)
            def _():
                halo_copy(step, piece).wait_send()

            @pl.when(gx > 0)
            def _():
                halo_copy(step, PIECES + piece).wait_send()

        halo_copy(step, 2 * PIECES).wait_send()
        for k in range(2 * REACH + 1):
            if k == REACH:
                continue
            away = REACH - k

            @pl.when((gx + away >= 0) & (gx + away < peers))
            def _():
                well_copy(step, k).wait_send()

    for step in range(1, everyone):
        dots_copy(step, me).wait_send()


def store(first, second, first_out, second_out, sem):
    copies = [
        pltpu.make_async_copy(first, first_out, sem.at[0]),
        pltpu.make_async_copy(second, second_out, sem.at[1]),
    ]
    for copy in copies:
        copy.start()
    for copy in copies:
        copy.wait()


def shards(peers, *args):
    rhs = args[0]
    _, width, height, depth = rhs.shape
    owned = args[-1].shape[-1]
    buckets = RING * owned
    rows = width * height
    everyone = peers * 2
    plane = (POWERS, 2, height, depth)
    wells = 2 * REACH + 1
    vmem = pl.BlockSpec(memory_space=pltpu.VMEM)
    results = pl.pallas_call(
        functools.partial(kernel, peers),
        out_shape=[jax.ShapeDtypeStruct(rhs.shape, F32)] * 2,
        in_specs=[pl.BlockSpec(memory_space=pl.ANY)] * len(args),
        out_specs=[vmem] * 2,
        scratch_shapes=[pltpu.VMEM(a.shape, a.dtype) for a in args]
        + [
            pltpu.SemaphoreType.DMA((len(args),)),
            pltpu.VMEM((POWERS, 2, width, height, depth), F32),
            pltpu.VMEM((POWERS, 2, width, height, depth), F32),
            pltpu.VMEM((2, width, height, depth), F32),
            pltpu.VMEM((rows, buckets), F32),
            pltpu.VMEM((wells, 8, 128), F32),
            pltpu.VMEM((4, 128), F32),
            pltpu.VMEM((8, 128), F32),
            pltpu.VMEM(plane, F32),
            pltpu.VMEM(plane, F32),
            pltpu.VMEM(plane, F32),
            pltpu.VMEM((POWERS, 2 * width, depth), F32),
            pltpu.VMEM((POWERS, 2 * width, depth), F32),
            pltpu.VMEM((POWERS, 8, 128), F32),
            pltpu.VMEM((POWERS, wells, 8, 128), F32),
            pltpu.VMEM((16, depth), F32),
            pltpu.VMEM((1, depth), F32),
            pltpu.VMEM((everyone, 1, depth), F32),
            pltpu.SemaphoreType.DMA((POWERS, 2 * PIECES + 1)),
            pltpu.SemaphoreType.DMA((POWERS, 2 * PIECES + 1)),
            pltpu.SemaphoreType.DMA((POWERS, wells)),
            pltpu.SemaphoreType.DMA((POWERS, wells)),
            pltpu.SemaphoreType.DMA((everyone,)),
            pltpu.SemaphoreType.DMA((everyone,)),
        ],
        compiler_params=pltpu.CompilerParams(
            collective_id=0, has_side_effects=True, vmem_limit_bytes=60 * 1024 * 1024
        ),
    )(*args)
    anywhere = pl.BlockSpec(memory_space=pl.ANY)
    return pl.pallas_call(
        store,
        out_shape=[jax.ShapeDtypeStruct(rhs.shape, F32)] * 2,
        in_specs=[vmem] * 2,
        out_specs=[anywhere] * 2,
        scratch_shapes=[pltpu.SemaphoreType.DMA((2,))],
    )(*results)


def solution(mesh):
    cell = P("ens", "gx", "gy", None)
    coupling = P("ens", None, "gx", "gy", None)
    tile = P(("ens", "gx"), "gy", None)
    in_specs = (cell,) * 3 + (coupling,) * 4 + (cell,) * 2 + (tile,) * 5
    return jax.shard_map(
        functools.partial(shards, mesh.shape["gx"]),
        mesh=mesh,
        in_specs=in_specs,
        out_specs=(cell, cell),
        check_vma=False,
    )
```
